128 devices in a mesh: row: 8 (over z, x_hi), col: 16 (over y, x_lo, core).
Axes of the slice: x: 4 (x_hi: 2, x_lo: 2; x = x_hi * 2 + x_lo), y: 4, z: 4, core: 2. Of those that a mesh axis runs over, the one named last changes fastest.
Arguments:
- residual: float32 [6144, 64000], P('row', 'col'), may hold values from -6 to 6
- cycle_coupling: float32 [6144, 1, 768], P('row', None, 'col'), may hold values from -0.21875 to 0.21875
- pair_amps: float32 [80, 614400], P(None, ('row', 'col')), may hold values from -6 to 6
- occupied_order: int32 [80], replicated, may hold values from 0 to 79, each once
- virtual_order: int32 [800], replicated, may hold values from 0 to 799, each once
Outputs:
- residual_out: float32 [6144, 64000], P('row', 'col')
The draws below stay inside these ranges and needn't reach their ends.
Inputs may be any that keep to these rules, and one draw needn't show every extreme that they name: `occupied_order`: every canonical occupied orbital appears once. `virtual_order`: every canonical virtual orbital appears once.
All inputs are finite; a program needn't handle non-finite values.
Results may differ from the reference program's by a relative error of at most 0.000051.
Values sent between devices are 32-bit elements; how exact they have to be, the bound alone decides.
A program may use at most 192 MiB of HBM per device.

```python
import jax
import jax.numpy as jnp
from jax import lax

NOCC = 80
NVIR = 800
KP = 1
CP = 768
ROWS = 6144
JB = 64000


def block_scale(stream_key, extent, pieces, least, largest):
    def one(dim, shards_of):
        draws = jax.random.uniform(jax.random.fold_in(jax.random.fold_in(stream_key, 6), dim), (shards_of,), jnp.float32, least / len(pieces), largest / len(pieces))
        return jnp.repeat(jnp.exp(draws), extent[dim] // shards_of).reshape((-1,) + (1,) * (len(extent) - dim - 1))

    gain = one(*pieces[0])
    for cut in pieces[1:]:
        gain = gain * one(*cut)
    return gain


def bell_draw(stream_key, dims, scale, reach, pieces=(), held_as=jnp.bfloat16):
    drawn = jax.random.normal(stream_key, dims, jnp.float32) * scale
    if len(pieces) > 0:
        drawn = block_scale(stream_key, dims, pieces, -0.22, 0.18) * drawn
    return jnp.clip(drawn, min=-reach, max=reach).astype(held_as)


def setup_inputs(seed: int = 0) -> dict:
    arg_keys = jax.random.split(jax.random.key(seed), 6)
    return {
        "residual": bell_draw(arg_keys[0], (ROWS, JB), 1.0, 6.0, ((0, 8), (1, 16)), jnp.float32),
        "cycle_coupling": bell_draw(arg_keys[1], (ROWS, KP, CP), (KP * CP) ** -0.5, 0.21875, ((0, 8), (2, 16)), jnp.float32),
        "pair_amps": bell_draw(arg_keys[2], (KP * NOCC, CP * NVIR), 1.0, 6.0, ((1, 128),), jnp.float32),
        "occupied_order": jax.random.permutation(arg_keys[3], NOCC).astype(jnp.int32),
        "virtual_order": jax.random.permutation(arg_keys[4], NVIR).astype(jnp.int32),
    }


def inverse_of(order, count):
    return jnp.zeros((count,), jnp.int32).at[order.astype(jnp.int32)].set(jnp.arange(count, dtype=jnp.int32))


def reference(residual, cycle_coupling, pair_amps, occupied_order, virtual_order):
    occupied_inverse = inverse_of(occupied_order, NOCC)
    virtual_inverse = inverse_of(virtual_order, NVIR)
    stored = pair_amps.reshape(KP, NOCC, CP, NVIR)
    panel = jnp.take(stored, occupied_inverse, axis=1)
    panel = jnp.take(panel, virtual_inverse, axis=3)
    panel = jnp.transpose(panel, (0, 2, 1, 3)).reshape(KP * CP, NOCC * NVIR)
    coupling = cycle_coupling.reshape(ROWS, KP * CP)
    update = jnp.dot(coupling, panel, precision=lax.Precision.HIGHEST, preferred_element_type=jnp.float32)
    return residual + update
```

```python
import functools

import jax
import jax.numpy as jnp
from jax import lax
from jax.experimental import pallas as pl
from jax.experimental.pallas import tpu as pltpu
from jax.sharding import PartitionSpec as P

F32 = jnp.float32
BF16 = jnp.bfloat16
MESH = pl.DeviceIdType.MESH

LANES = 512
LAG_PERMUTE = -2
LAG_REGROUP = 0
LAG_FIRST = 1
LAG_SECOND = 2
LAG_MATMUL = 3

REGROUP, ACROSS, LOW, HIGH, FAR_LOW, FAR_HIGH, MIX_LOW, MIX_HIGH, MIXFAR_LOW, MIXFAR_HIGH = range(10)
EDGE_LOW, EDGE_HIGH, EDGE_FAR_LOW, EDGE_FAR_HIGH = range(10, 14)
KINDS = 14
W_ACROSS, W_ALONG, W_CORE = range(3)


def split(x):
    high = x.astype(BF16)
    return high, (x - high.astype(F32)).astype(BF16)


def kernel(
    chunks,
    occupied_ref,
    virtual_ref,
    amps_hbm,
    coupling_hbm,
    residual_ref,
    out_ref,
    amps,
    coupling_in,
    stored,
    picked,
    outgoing,
    incoming,
    panel,
    coupling_t,
    weights,
    factors,
    load_sem,
    send_sem,
    recv_sem,
    w_send_sem,
    w_recv_sem,
):
    step = pl.program_id(0)
    row = lax.axis_index("row")
    col = lax.axis_index("col")
    z, hi = row // 2, row % 2
    up, down, far = (z + 1) % 4, (z + 3) % 4, (z + 2) % 4
    across = (z * 2 + 1 - hi, col)
    above = (up * 2 + hi, col)
    below = (down * 2 + hi, col)
    width = LANES
    block = panel.shape[0] // 8
    blocks, virtual = picked.shape[0], picked.shape[2]
    cut = block // 6
    half = block // 2

    def lanes(chunk):
        return pl.ds(pl.multiple_of(chunk * width, width), width)

    def remote(src, dst, kind, chunk, where):
        pltpu.make_async_remote_copy(
            src_ref=src,
            dst_ref=dst,
            send_sem=send_sem.at[kind],
            recv_sem=recv_sem.at[chunk, kind],
            device_id=where,
            device_id_type=MESH,
        ).start()

    def rows(owner_z, owner_hi, first, count):
        start = (owner_z * 2 + owner_hi) * block + first
        return pl.ds(pl.multiple_of(start, 16), count)

    def push(owner_z, owner_hi, first, count, kind, chunk, where):
        ref = panel.at[rows(owner_z, owner_hi, first, count), lanes(chunk)]
        remote(ref, ref, kind, chunk, where)

    def arrived(kind, chunk, count):
        ref = panel.at[pl.ds(0, count), lanes(chunk)]
        pltpu.make_async_copy(ref, ref, recv_sem.at[chunk, kind]).wait()

    def pick(j):
        shape = (128, 480)
        r = lax.broadcasted_iota(jnp.int32, shape, 0)
        k = lax.broadcasted_iota(jnp.int32, shape, 1)
        wanted = jnp.where(r % 8 == k // 80, (r // 8) * blocks + j, -1)
        order = jnp.concatenate([occupied_ref[...]] * 6, axis=1)
        one_hot = (wanted == order).astype(F32).astype(BF16)
        for s in range(2):
            picked[j, pl.ds(128 * s, 128), :] = jnp.dot(
                one_hot, stored[s], preferred_element_type=F32
            ).astype(BF16)

    def permute(chunk, spanned=2):
        shape = (width, virtual)
        lane = lax.broadcasted_iota(jnp.int32, shape, 0) + chunk * width
        first = (chunk * width) // virtual
        total = jnp.zeros((256, width), F32)
        for n in range(spanned):
            j = jnp.minimum(first + n, blocks - 1)
            target = virtual_ref[...] + (first + n) * virtual
            one_hot = (lane == target).astype(F32).astype(BF16)
            total += lax.dot_general(
                picked[j], one_hot, (((1,), (1,)), ((), ())), preferred_element_type=F32
            )
        values = (total[:128] + total[128:]).reshape(16, 8, width)
        outgoing[:, :, lanes(chunk)] = values
        incoming[col, :, lanes(chunk)] = outgoing[col, :, lanes(chunk)]
        for d in range(1, 16):
            other = (col + d) % 16
            remote(
                outgoing.at[other, pl.ds(0, 6), lanes(chunk)],
                incoming.at[col, pl.ds(0, 6), lanes(chunk)],
                REGROUP,
                chunk,
                (row, other),
            )

    partners = [across, above, below]

    @pl.when(step == 0)
    def _():
        load_amps = pltpu.make_async_copy(amps_hbm, amps, load_sem.at[0])
        load_amps.start()
        load_coupling = pltpu.make_async_copy(coupling_hbm, coupling_in, load_sem.at[1])
        load_coupling.start()
        barrier = pltpu.get_barrier_semaphore()
        for where in partners:
            pl.semaphore_signal(barrier, inc=1, device_id=where, device_id_type=MESH)
        for d in range(1, 16):
            pl.semaphore_signal(barrier, inc=1, device_id=(row, (col + d) % 16), device_id_type=MESH)
        load_amps.wait()
        for i in range(6):
            high, low = split(amps[:, i * virtual : (i + 1) * virtual])
            stored[0, pl.ds(80 * i, 80), :] = high
            stored[1, pl.ds(80 * i, 80), :] = low
        pick(0)
        pl.semaphore_wait(barrier, 18)
        permute(0, pl.cdiv(width, virtual))
        load_coupling.wait()
        own = pl.ds(pl.multiple_of(col * 48, 16), 48)
        coupling_t[own, :] = coupling_in[...].reshape(768, 48).T
        pltpu.make_async_remote_copy(
            src_ref=coupling_t.at[own],
            dst_ref=coupling_t.at[own],
            send_sem=w_send_sem.at[W_ACROSS],
            recv_sem=w_recv_sem.at[W_ACROSS],
            device_id=(row, col // 4 * 4 + (col + 2) % 4),
            device_id_type=MESH,
        ).start()
        for j in range(1, blocks):
            pick(j)
        permute(1)

    def w_wait(sems, kind, count):
        ref = coupling_t.at[pl.ds(0, count)]
        pltpu.make_async_copy(ref, ref, sems.at[kind]).wait()

    def w_send(owner, kind, where):
        ref = coupling_t.at[pl.ds(pl.multiple_of(owner * 48, 16), 48)]
        pltpu.make_async_remote_copy(
            src_ref=ref,
            dst_ref=ref,
            send_sem=w_send_sem.at[kind],
            recv_sem=w_recv_sem.at[kind],
            device_id=where,
            device_id_type=MESH,
        ).start()

    chunk_r = step - LAG_REGROUP

    @pl.when((chunk_r >= 0) & (chunk_r < chunks))
    def _():
        ref = incoming.at[pl.ds(0, 15), pl.ds(0, 6), lanes(chunk_r)]
        pltpu.make_async_copy(ref, ref, recv_sem.at[chunk_r, REGROUP]).wait()
        pieces = [incoming[q, :, lanes(chunk_r)][:6] for q in range(16)]
        panel[rows(z, hi, 0, block), lanes(chunk_r)] = jnp.concatenate(pieces, axis=0)
        push(z, hi, 0, block, ACROSS, chunk_r, across)
        push(z, hi, 0, block, LOW, chunk_r, above)
        push(z, hi, 0, block, HIGH, chunk_r, below)

    chunk_f = step - LAG_FIRST

    @pl.when((chunk_f >= 0) & (chunk_f < chunks))
    def _():
        arrived(ACROSS, chunk_f, block)
        push(z, 1 - hi, cut, block - 2 * cut, MIX_LOW, chunk_f, above)
        push(z, 1 - hi, cut, block - 2 * cut, MIX_HIGH, chunk_f, below)
        arrived(LOW, chunk_f, block)
        push(down, hi, 0, half, FAR_LOW, chunk_f, above)
        push(down, hi, 0, cut, EDGE_LOW, chunk_f, across)
        push(down, hi, block - cut, cut, EDGE_LOW, chunk_f, across)
        arrived(HIGH, chunk_f, block)
        push(up, hi, half, half, FAR_HIGH, chunk_f, below)
        push(up, hi, 0, cut, EDGE_HIGH, chunk_f, across)
        push(up, hi, block - cut, cut, EDGE_HIGH, chunk_f, across)

    chunk_s = step - LAG_SECOND

    @pl.when((chunk_s >= 0) & (chunk_s < chunks))
    def _():
        arrived(MIX_LOW, chunk_s, block - 2 * cut)
        push(down, 1 - hi, cut, half - cut, MIXFAR_LOW, chunk_s, above)
        arrived(MIX_HIGH, chunk_s, block - 2 * cut)
        push(up, 1 - hi, half, half - cut, MIXFAR_HIGH, chunk_s, below)
        arrived(FAR_LOW, chunk_s, half)
        push(far, hi, 0, cut, EDGE_FAR_LOW, chunk_s, across)
        arrived(FAR_HIGH, chunk_s, half)
        push(far, hi, block - cut, cut, EDGE_FAR_HIGH, chunk_s, across)

    chunk_p = step - LAG_PERMUTE

    @pl.when(chunk_p < chunks)
    def _():
        permute(chunk_p)

    @pl.when(step == 1)
    def _():
        w_wait(w_recv_sem, W_ACROSS, 48)
        for d in range(1, 4):
            where = (row, (col + 4 * d) % 16)
            w_send(col, W_ALONG, where)
            w_send(col // 4 * 4 + (col + 2) % 4, W_ALONG, where)

    @pl.when(step == 2)
    def _():
        w_wait(w_recv_sem, W_ALONG, 48 * 6)
        where = (row, col // 2 * 2 + 1 - col % 2)
        for n in range(8):
            w_send(n * 2 + col % 2, W_CORE, where)

    @pl.when(step == LAG_MATMUL)
    def _():
        w_wait(w_recv_sem, W_CORE, 48 * 8)
        size = coupling_t.shape[0]
        high, low = split(coupling_t[...].T)
        weights[:, 0:size] = high
        weights[:, size : 2 * size] = low
        weights[:, 2 * size : 3 * size] = high

    chunk_m = step - LAG_MATMUL

    @pl.when(chunk_m >= 0)
    def _():
        arrived(EDGE_LOW, chunk_m, 2 * cut)
        arrived(EDGE_HIGH, chunk_m, 2 * cut)
        arrived(EDGE_FAR_LOW, chunk_m, cut)
        arrived(EDGE_FAR_HIGH, chunk_m, cut)
        arrived(MIXFAR_LOW, chunk_m, half - cut)
        arrived(MIXFAR_HIGH, chunk_m, half - cut)
        size = panel.shape[0]
        high, low = split(panel[:, lanes(chunk_m)])
        factors[0:size] = high
        factors[size : 2 * size] = high
        factors[2 * size : 3 * size] = low
        out_ref[...] = residual_ref[...] + jnp.dot(
            weights[...], factors[...], preferred_element_type=F32
        )

    @pl.when(step == pl.num_programs(0) - 1)
    def _():
        everything = pl.ds(0, chunks * width)
        ref = incoming.at[pl.ds(0, 15), pl.ds(0, 6), everything]
        pltpu.make_async_copy(ref, ref, send_sem.at[REGROUP]).wait()
        counts = {ACROSS: block, LOW: block, HIGH: block, FAR_LOW: half, FAR_HIGH: half}
        counts |= {MIX_LOW: block - 2 * cut, MIX_HIGH: block - 2 * cut, MIXFAR_LOW: half - cut}
        counts |= {MIXFAR_HIGH: half - cut, EDGE_LOW: 2 * cut, EDGE_HIGH: 2 * cut}
        counts |= {EDGE_FAR_LOW: cut, EDGE_FAR_HIGH: cut}
        for kind, count in counts.items():
            ref = panel.at[pl.ds(0, count), everything]
            pltpu.make_async_copy(ref, ref, send_sem.at[kind]).wait()
        w_wait(w_send_sem, W_ACROSS, 48)
        w_wait(w_send_sem, W_ALONG, 48 * 6)
        w_wait(w_send_sem, W_CORE, 48 * 8)


def shards(residual, cycle_coupling, pair_amps, occupied_order, virtual_order):
    occupied = occupied_order.shape[0]
    virtual = virtual_order.shape[0]
    local_rows, local_columns = residual.shape
    depth = local_rows
    chunks = pl.cdiv(local_columns, LANES)
    padded = chunks * LANES
    columns = local_columns // virtual
    steps = chunks + LAG_MATMUL

    def at(step):
        return 0, jnp.maximum(step - LAG_MATMUL, 0)

    def whole(shape):
        return pl.BlockSpec(shape, lambda step: (0, 0))

    anywhere = pl.BlockSpec(memory_space=pl.ANY)
    return pl.pallas_call(
        functools.partial(kernel, chunks),
        grid=(steps,),
        out_shape=jax.ShapeDtypeStruct(residual.shape, F32),
        in_specs=[
            whole((1, occupied)),
            whole((1, virtual)),
            anywhere,
            anywhere,
            pl.BlockSpec((local_rows, LANES), at),
        ],
        out_specs=pl.BlockSpec((local_rows, LANES), at),
        scratch_shapes=[
            pltpu.VMEM(pair_amps.shape, F32),
            pltpu.VMEM(cycle_coupling.shape, F32),
            pltpu.VMEM((2, 6 * occupied, virtual), BF16),
            pltpu.VMEM((columns, 256, virtual), BF16),
            pltpu.VMEM((16, 8, padded), F32),
            pltpu.VMEM((16, 8, padded), F32),
            pltpu.VMEM((depth, padded), F32),
            pltpu.VMEM((depth, local_rows), F32),
            pltpu.VMEM((local_rows, 3 * depth), BF16),
            pltpu.VMEM((3 * depth, LANES), BF16),
            pltpu.SemaphoreType.DMA((2,)),
            pltpu.SemaphoreType.DMA((KINDS,)),
            pltpu.SemaphoreType.DMA((chunks, KINDS)),
            pltpu.SemaphoreType.DMA((3,)),
            pltpu.SemaphoreType.DMA((3,)),
        ],
        compiler_params=pltpu.CompilerParams(
            collective_id=0, has_side_effects=True, vmem_limit_bytes=60 * 2**20
        ),
        cost_estimate=pl.CostEstimate(
            flops=6 * local_rows * depth * local_columns,
            bytes_accessed=8 * local_rows * local_columns,
            transcendentals=0,
        ),
    )(
        occupied_order.reshape(1, occupied),
        virtual_order.reshape(1, virtual),
        pair_amps,
        cycle_coupling,
        residual,
    )


def solution(mesh):
    in_specs = (P("row", "col"), P("row", None, "col"), P(None, ("row", "col")), P(), P())
    out_specs = P("row", "col")
    return jax.shard_map(shards, mesh=mesh, in_specs=in_specs, out_specs=out_specs, check_vma=False)
```

```python
import functools

import jax
import jax.numpy as jnp
from jax import lax
from jax.experimental import pallas as pl
from jax.experimental.pallas import tpu as pltpu
from jax.sharding import PartitionSpec as P

F32 = jnp.float32
BF16 = jnp.bfloat16
MESH = pl.DeviceIdType.MESH

LANES = 512
LAG_PERMUTE = -2
LAG_REGROUP = 0
LAG_FIRST = 1
LAG_SECOND = 2
LAG_MATMUL = 3

REGROUP, ACROSS, LOW, HIGH, FAR_LOW, FAR_HIGH, MIX_LOW, MIX_HIGH, MIXFAR_LOW, MIXFAR_HIGH = range(10)
EDGE_LOW, EDGE_HIGH, EDGE_FAR_LOW, EDGE_FAR_HIGH = range(10, 14)
KINDS = 14
W_ACROSS, W_ALONG, W_CORE = range(3)


def split(x):
    high = x.astype(BF16)
    return high, (x - high.astype(F32)).astype(BF16)


def kernel(
    chunks,
    occupied_ref,
    virtual_ref,
    amps_hbm,
    coupling_hbm,
    residual_ref,
    out_ref,
    amps,
    stored,
    picked,
    outgoing,
    incoming,
    panel,
    coupling_t,
    weights,
    factors,
    load_sem,
    send_sem,
    recv_sem,
    w_send_sem,
    w_recv_sem,
):
    step = pl.program_id(0)
    row = lax.axis_index("row")
    col = lax.axis_index("col")
    z, hi = row // 2, row % 2
    up, down, far = (z + 1) % 4, (z + 3) % 4, (z + 2) % 4
    across = (z * 2 + 1 - hi, col)
    above = (up * 2 + hi, col)
    below = (down * 2 + hi, col)
    width = LANES
    block = panel.shape[0] // 8
    blocks, virtual = picked.shape[0], picked.shape[2]
    cut = block // 6
    half = block // 2

    def lanes(chunk):
        return pl.ds(pl.multiple_of(chunk * width, width), width)

    def remote(src, dst, kind, chunk, where):
        pltpu.make_async_remote_copy(
            src_ref=src,
            dst_ref=dst,
            send_sem=send_sem.at[kind],
            recv_sem=recv_sem.at[chunk, kind],
            device_id=where,
            device_id_type=MESH,
        ).start()

    def rows(owner_z, owner_hi, first, count):
        start = (owner_z * 2 + owner_hi) * block + first
        return pl.ds(pl.multiple_of(start, 16), count)

    def push(owner_z, owner_hi, first, count, kind, chunk, where):
        ref = panel.at[rows(owner_z, owner_hi, first, count), lanes(chunk)]
        remote(ref, ref, kind, chunk, where)

    def arrived(kind, chunk, count):
        ref = panel.at[pl.ds(0, count), lanes(chunk)]
        pltpu.make_async_copy(ref, ref, recv_sem.at[chunk, kind]).wait()

    def pick(j):
        shape = (128, 480)
        r = lax.broadcasted_iota(jnp.int32, shape, 0)
        k = lax.broadcasted_iota(jnp.int32, shape, 1)
        wanted = jnp.where(r % 8 == k // 80, (r // 8) * blocks + j, -1)
        order = jnp.concatenate([occupied_ref[...]] * 6, axis=1)
        one_hot = (wanted == order).astype(F32).astype(BF16)
        for s in range(2):
            picked[j, pl.ds(128 * s, 128), :] = jnp.dot(
                one_hot, stored[s], preferred_element_type=F32
            ).astype(BF16)

    def permute(chunk, spanned=2):
        shape = (width, virtual)
        lane = lax.broadcasted_iota(jnp.int32, shape, 0) + chunk * width
        first = (chunk * width) // virtual
        total = jnp.zeros((256, width), F32)
        for n in range(spanned):
            j = jnp.minimum(first + n, blocks - 1)
            target = virtual_ref[...] + (first + n) * virtual
            one_hot = (lane == target).astype(F32).astype(BF16)
            total += lax.dot_general(
                picked[j], one_hot, (((1,), (1,)), ((), ())), preferred_element_type=F32
            )
        values = (total[:128] + total[128:]).reshape(16, 8, width)
        outgoing[:, :, lanes(chunk)] = values
        incoming[col, :, lanes(chunk)] = outgoing[col, :, lanes(chunk)]
        for d in range(1, 16):
            other = (col + d) % 16
            remote(
                outgoing.at[other, pl.ds(0, 6), lanes(chunk)],
                incoming.at[col, pl.ds(0, 6), lanes(chunk)],
                REGROUP,
                chunk,
                (row, other),
            )

    partners = [across, above, below]

    @pl.when(step == 0)
    def _():
        load_amps = pltpu.make_async_copy(amps_hbm, amps, load_sem.at[0])
        load_amps.start()
        own = pl.ds(pl.multiple_of(col * 48, 16), 48)
        load_coupling = pltpu.make_async_copy(coupling_hbm, coupling_t.at[own], load_sem.at[1])
        load_coupling.start()
        barrier = pltpu.get_barrier_semaphore()
        for where in partners:
            pl.semaphore_signal(barrier, inc=1, device_id=where, device_id_type=MESH)
        for d in range(1, 16):
            pl.semaphore_signal(barrier, inc=1, device_id=(row, (col + d) % 16), device_id_type=MESH)
        load_amps.wait()
        for i in range(6):
            high, low = split(amps[:, i * virtual : (i + 1) * virtual])
            stored[0, pl.ds(80 * i, 80), :] = high
            stored[1, pl.ds(80 * i, 80), :] = low
        pick(0)
        pl.semaphore_wait(barrier, 18)
        permute(0, pl.cdiv(width, virtual))
        load_coupling.wait()
        pltpu.make_async_remote_copy(
            src_ref=coupling_t.at[own],
            dst_ref=coupling_t.at[own],
            send_sem=w_send_sem.at[W_ACROSS],
            recv_sem=w_recv_sem.at[W_ACROSS],
            device_id=(row, col // 4 * 4 + (col + 2) % 4),
            device_id_type=MESH,
        ).start()
        for j in range(1, blocks):
            pick(j)
        permute(1)

    def w_wait(sems, kind, count):
        ref = coupling_t.at[pl.ds(0, count)]
        pltpu.make_async_copy(ref, ref, sems.at[kind]).wait()

    def w_send(owner, kind, where):
        ref = coupling_t.at[pl.ds(pl.multiple_of(owner * 48, 16), 48)]
        pltpu.make_async_remote_copy(
            src_ref=ref,
            dst_ref=ref,
            send_sem=w_send_sem.at[kind],
            recv_sem=w_recv_sem.at[kind],
            device_id=where,
            device_id_type=MESH,
        ).start()

    chunk_r = step - LAG_REGROUP

    @pl.when((chunk_r >= 0) & (chunk_r < chunks))
    def _():
        ref = incoming.at[pl.ds(0, 15), pl.ds(0, 6), lanes(chunk_r)]
        pltpu.make_async_copy(ref, ref, recv_sem.at[chunk_r, REGROUP]).wait()
        pieces = [incoming[q, :, lanes(chunk_r)][:6] for q in range(16)]
        panel[rows(z, hi, 0, block), lanes(chunk_r)] = jnp.concatenate(pieces, axis=0)
        push(z, hi, 0, block, ACROSS, chunk_r, across)
        push(z, hi, 0, block, LOW, chunk_r, above)
        push(z, hi, 0, block, HIGH, chunk_r, below)

    chunk_f = step - LAG_FIRST

    @pl.when((chunk_f >= 0) & (chunk_f < chunks))
    def _():
        arrived(ACROSS, chunk_f, block)
        push(z, 1 - hi, cut, block - 2 * cut, MIX_LOW, chunk_f, above)
        push(z, 1 - hi, cut, block - 2 * cut, MIX_HIGH, chunk_f, below)
        arrived(LOW, chunk_f, block)
        push(down, hi, 0, half, FAR_LOW, chunk_f, above)
        push(down, hi, 0, cut, EDGE_LOW, chunk_f, across)
        push(down, hi, block - cut, cut, EDGE_LOW, chunk_f, across)
        arrived(HIGH, chunk_f, block)
        push(up, hi, half, half, FAR_HIGH, chunk_f, below)
        push(up, hi, 0, cut, EDGE_HIGH, chunk_f, across)
        push(up, hi, block - cut, cut, EDGE_HIGH, chunk_f, across)

    chunk_s = step - LAG_SECOND

    @pl.when((chunk_s >= 0) & (chunk_s < chunks))
    def _():
        arrived(MIX_LOW, chunk_s, block - 2 * cut)
        push(down, 1 - hi, cut, half - cut, MIXFAR_LOW, chunk_s, above)
        arrived(MIX_HIGH, chunk_s, block - 2 * cut)
        push(up, 1 - hi, half, half - cut, MIXFAR_HIGH, chunk_s, below)
        arrived(FAR_LOW, chunk_s, half)
        push(far, hi, 0, cut, EDGE_FAR_LOW, chunk_s, across)
        arrived(FAR_HIGH, chunk_s, half)
        push(far, hi, block - cut, cut, EDGE_FAR_HIGH, chunk_s, across)

    chunk_p = step - LAG_PERMUTE

    @pl.when(chunk_p < chunks)
    def _():
        permute(chunk_p)

    @pl.when(step == 1)
    def _():
        w_wait(w_recv_sem, W_ACROSS, 48)
        for d in range(1, 4):
            where = (row, (col + 4 * d) % 16)
            w_send(col, W_ALONG, where)
            w_send(col // 4 * 4 + (col + 2) % 4, W_ALONG, where)

    @pl.when(step == 2)
    def _():
        w_wait(w_recv_sem, W_ALONG, 48 * 6)
        where = (row, col // 2 * 2 + 1 - col % 2)
        for n in range(8):
            w_send(n * 2 + col % 2, W_CORE, where)

    @pl.when(step == LAG_MATMUL)
    def _():
        w_wait(w_recv_sem, W_CORE, 48 * 8)
        size = coupling_t.shape[0]
        high, low = split(coupling_t[...])
        weights[0:size] = high
        weights[size : 2 * size] = low
        weights[2 * size : 3 * size] = high

    chunk_m = step - LAG_MATMUL

    @pl.when(chunk_m >= 0)
    def _():
        arrived(EDGE_LOW, chunk_m, 2 * cut)
        arrived(EDGE_HIGH, chunk_m, 2 * cut)
        arrived(EDGE_FAR_LOW, chunk_m, cut)
        arrived(EDGE_FAR_HIGH, chunk_m, cut)
        arrived(MIXFAR_LOW, chunk_m, half - cut)
        arrived(MIXFAR_HIGH, chunk_m, half - cut)
        size = panel.shape[0]
        high, low = split(panel[:, lanes(chunk_m)].T)
        factors[:, 0:size] = high
        factors[:, size : 2 * size] = high
        factors[:, 2 * size : 3 * size] = low
        out_ref[...] = residual_ref[...] + jnp.dot(
            factors[...], weights[...], preferred_element_type=F32
        )

    @pl.when(step == pl.num_programs(0) - 1)
    def _():
        everything = pl.ds(0, chunks * width)
        ref = incoming.at[pl.ds(0, 15), pl.ds(0, 6), everything]
        pltpu.make_async_copy(ref, ref, send_sem.at[REGROUP]).wait()
        counts = {ACROSS: block, LOW: block, HIGH: block, FAR_LOW: half, FAR_HIGH: half}
        counts |= {MIX_LOW: block - 2 * cut, MIX_HIGH: block - 2 * cut, MIXFAR_LOW: half - cut}
        counts |= {MIXFAR_HIGH: half - cut, EDGE_LOW: 2 * cut, EDGE_HIGH: 2 * cut}
        counts |= {EDGE_FAR_LOW: cut, EDGE_FAR_HIGH: cut}
        for kind, count in counts.items():
            ref = panel.at[pl.ds(0, count), everything]
            pltpu.make_async_copy(ref, ref, send_sem.at[kind]).wait()
        w_wait(w_send_sem, W_ACROSS, 48)
        w_wait(w_send_sem, W_ALONG, 48 * 6)
        w_wait(w_send_sem, W_CORE, 48 * 8)


def shards(residual, cycle_coupling, pair_amps, occupied_order, virtual_order):
    occupied = occupied_order.shape[0]
    virtual = virtual_order.shape[0]
    local_rows, local_columns = residual.shape
    residual = residual.T
    coupling = cycle_coupling.reshape(local_rows, cycle_coupling.shape[2]).T
    depth = local_rows
    chunks = pl.cdiv(local_columns, LANES)
    padded = chunks * LANES
    columns = local_columns // virtual
    steps = chunks + LAG_MATMUL

    def at(step):
        return jnp.maximum(step - LAG_MATMUL, 0), 0

    def whole(shape):
        return pl.BlockSpec(shape, lambda step: (0, 0))

    anywhere = pl.BlockSpec(memory_space=pl.ANY)
    return pl.pallas_call(
        functools.partial(kernel, chunks),
        grid=(steps,),
        out_shape=jax.ShapeDtypeStruct(residual.shape, F32),
        in_specs=[
            whole((1, occupied)),
            whole((1, virtual)),
            anywhere,
            anywhere,
            pl.BlockSpec((LANES, local_rows), at),
        ],
        out_specs=pl.BlockSpec((LANES, local_rows), at),
        scratch_shapes=[
            pltpu.VMEM(pair_amps.shape, F32),
            pltpu.VMEM((2, 6 * occupied, virtual), BF16),
            pltpu.VMEM((columns, 256, virtual), BF16),
            pltpu.VMEM((16, 8, padded), F32),
            pltpu.VMEM((16, 8, padded), F32),
            pltpu.VMEM((depth, padded), F32),
            pltpu.VMEM((depth, local_rows), F32),
            pltpu.VMEM((3 * depth, local_rows), BF16),
            pltpu.VMEM((LANES, 3 * depth), BF16),
            pltpu.SemaphoreType.DMA((2,)),
            pltpu.SemaphoreType.DMA((KINDS,)),
            pltpu.SemaphoreType.DMA((chunks, KINDS)),
            pltpu.SemaphoreType.DMA((3,)),
            pltpu.SemaphoreType.DMA((3,)),
        ],
        compiler_params=pltpu.CompilerParams(
            collective_id=0, has_side_effects=True, vmem_limit_bytes=60 * 2**20
        ),
        cost_estimate=pl.CostEstimate(
            flops=6 * local_rows * depth * local_columns,
            bytes_accessed=8 * local_rows * local_columns,
            transcendentals=0,
        ),
    )(
        occupied_order.reshape(1, occupied),
        virtual_order.reshape(1, virtual),
        pair_amps,
        coupling,
        residual,
    ).T


def solution(mesh):
    in_specs = (P("row", "col"), P("row", None, "col"), P(None, ("row", "col")), P(), P())
    out_specs = P("row", "col")
    return jax.shard_map(shards, mesh=mesh, in_specs=in_specs, out_specs=out_specs, check_vma=False)
```

```python
import functools

import jax
import jax.numpy as jnp
from jax import lax
from jax.experimental import pallas as pl
from jax.experimental.pallas import tpu as pltpu
from jax.sharding import PartitionSpec as P

F32 = jnp.float32
BF16 = jnp.bfloat16
MESH = pl.DeviceIdType.MESH

LANES = 512
LAG_REGROUP = 0
LAG_FIRST = 1
LAG_SECOND = 2
LAG_MATMUL = 3

REGROUP, ACROSS, LOW, HIGH, FAR_LOW, FAR_HIGH, MIX_LOW, MIX_HIGH, MIXFAR_LOW, MIXFAR_HIGH = range(10)
EDGE_LOW, EDGE_HIGH, EDGE_FAR = range(10, 13)
KINDS = 13
GROUPS = {first: 1 for first in range(8)}
W_ACROSS, W_ALONG, W_CORE = range(3)


def split(x):
    high = x.astype(BF16)
    return high, (x - high.astype(F32)).astype(BF16)


def kernel(
    chunks,
    occupied_ref,
    virtual_ref,
    amps_hbm,
    coupling_hbm,
    residual_ref,
    out_hbm,
    amps,
    stored,
    picked,
    outgoing,
    incoming,
    panel,
    coupling_t,
    weights,
    factors,
    results,
    load_sem,
    store_sem,
    send_sem,
    recv_sem,
    w_send_sem,
    w_recv_sem,
):
    step = pl.program_id(0)
    row = lax.axis_index("row")
    col = lax.axis_index("col")
    z, hi = row // 2, row % 2
    up, down, far = (z + 1) % 4, (z + 3) % 4, (z + 2) % 4
    across = (z * 2 + 1 - hi, col)
    above = (up * 2 + hi, col)
    below = (down * 2 + hi, col)
    width = LANES
    block = panel.shape[0] // 8
    blocks, virtual = picked.shape[0], picked.shape[2]
    cut = block // 3
    mixed = block - cut
    half = block // 2
    middle = cut + mixed // 2

    def lanes(chunk):
        return pl.ds(pl.multiple_of(chunk * width, width), width)

    def remote(src, dst, kind, chunk, where):
        pltpu.make_async_remote_copy(
            src_ref=src,
            dst_ref=dst,
            send_sem=send_sem.at[kind],
            recv_sem=recv_sem.at[chunk, kind],
            device_id=where,
            device_id_type=MESH,
        ).start()

    def rows(owner_z, owner_hi, first, count):
        start = (owner_z * 2 + owner_hi) * block + first
        return pl.ds(pl.multiple_of(start, 16), count)

    def push(owner_z, owner_hi, first, count, kind, chunk, where):
        ref = panel.at[rows(owner_z, owner_hi, first, count), lanes(chunk)]
        remote(ref, ref, kind, chunk, where)

    def arrived(kind, chunk, count):
        ref = panel.at[pl.ds(0, count), lanes(chunk)]
        pltpu.make_async_copy(ref, ref, recv_sem.at[chunk, kind]).wait()

    def pick(j):
        shape = (128, 480)
        r = lax.broadcasted_iota(jnp.int32, shape, 0)
        k = lax.broadcasted_iota(jnp.int32, shape, 1)
        wanted = jnp.where(r % 8 == k // 80, (r // 8) * blocks + j, -1)
        order = jnp.concatenate([occupied_ref[...]] * 6, axis=1)
        one_hot = (wanted == order).astype(F32).astype(BF16)
        for s in range(2):
            picked[j, pl.ds(128 * s, 128), :] = jnp.dot(
                one_hot, stored[s], preferred_element_type=F32
            ).astype(BF16)

    def permute(chunk, spanned=2):
        shape = (width, virtual)
        lane = lax.broadcasted_iota(jnp.int32, shape, 0) + chunk * width
        first = (chunk * width) // virtual
        total = jnp.zeros((256, width), F32)
        for n in range(spanned):
            j = jnp.minimum(first + n, blocks - 1)
            target = virtual_ref[...].reshape(1, virtual) + (first + n) * virtual
            one_hot = (lane == target).astype(F32).astype(BF16)
            total += lax.dot_general(
                picked[j], one_hot, (((1,), (1,)), ((), ())), preferred_element_type=F32
            )
        values = (total[:128] + total[128:]).reshape(16, 8, width)
        outgoing[:, :, lanes(chunk)] = values
        incoming[col, :, lanes(chunk)] = outgoing[col, :, lanes(chunk)]

    def group_lanes(first):
        return pl.ds(first * width, GROUPS[first] * width)

    def regroup(first):
        for d in range(1, 16):
            other = (col + d) % 16
            remote(
                outgoing.at[other, pl.ds(0, 6), group_lanes(first)],
                incoming.at[col, pl.ds(0, 6), group_lanes(first)],
                REGROUP,
                first,
                (row, other),
            )

    partners = [across, above, below]

    @pl.when(step == 0)
    def _():
        load_amps = pltpu.make_async_copy(amps_hbm, amps, load_sem.at[0])
        load_amps.start()
        own = pl.ds(pl.multiple_of(col * 48, 16), 48)
        load_coupling = pltpu.make_async_copy(coupling_hbm, coupling_t.at[own], load_sem.at[1])
        load_coupling.start()
        barrier = pltpu.get_barrier_semaphore()
        for where in partners:
            pl.semaphore_signal(barrier, inc=1, device_id=where, device_id_type=MESH)
        for d in range(1, 16):
            pl.semaphore_signal(barrier, inc=1, device_id=(row, (col + d) % 16), device_id_type=MESH)
        load_amps.wait()
        for i in range(6):
            high, low = split(amps[:, i * virtual : (i + 1) * virtual])
            stored[0, pl.ds(80 * i, 80), :] = high
            stored[1, pl.ds(80 * i, 80), :] = low
        pick(0)
        permute(0, pl.cdiv(width, virtual))
        pl.semaphore_wait(barrier, 18)
        regroup(0)
        load_coupling.wait()
        pltpu.make_async_remote_copy(
            src_ref=coupling_t.at[own],
            dst_ref=coupling_t.at[own],
            send_sem=w_send_sem.at[W_ACROSS],
            recv_sem=w_recv_sem.at[W_ACROSS],
            device_id=(row, col // 4 * 4 + (col + 2) % 4),
            device_id_type=MESH,
        ).start()
        pick(1)
        permute(1)
        regroup(1)

    def w_wait(sems, kind, count):
        ref = coupling_t.at[pl.ds(0, count)]
        pltpu.make_async_copy(ref, ref, sems.at[kind]).wait()

    def w_send(owner, kind, where):
        ref = coupling_t.at[pl.ds(pl.multiple_of(owner * 48, 16), 48)]
        pltpu.make_async_remote_copy(
            src_ref=ref,
            dst_ref=ref,
            send_sem=w_send_sem.at[kind],
            recv_sem=w_recv_sem.at[kind],
            device_id=where,
            device_id_type=MESH,
        ).start()

    chunk_r = step - LAG_REGROUP

    @pl.when((chunk_r >= 0) & (chunk_r < chunks))
    def _():
        for first in GROUPS:

            @pl.when(chunk_r == first)
            def _(first=first):
                ref = incoming.at[pl.ds(0, 15), pl.ds(0, 6), group_lanes(first)]
                pltpu.make_async_copy(ref, ref, recv_sem.at[first, REGROUP]).wait()

        pieces = [incoming[q, :, lanes(chunk_r)][:6] for q in range(16)]
        panel[rows(z, hi, 0, block), lanes(chunk_r)] = jnp.concatenate(pieces, axis=0)
        push(z, hi, 0, block, ACROSS, chunk_r, across)
        push(z, hi, 0, block, LOW, chunk_r, above)
        push(z, hi, 0, block, HIGH, chunk_r, below)

    chunk_f = step - LAG_FIRST

    @pl.when((chunk_f >= 0) & (chunk_f < chunks))
    def _():
        arrived(ACROSS, chunk_f, block)
        push(z, 1 - hi, cut, mixed, MIX_LOW, chunk_f, above)
        push(z, 1 - hi, cut, mixed, MIX_HIGH, chunk_f, below)
        arrived(LOW, chunk_f, block)
        push(down, hi, 0, half, FAR_LOW, chunk_f, above)
        push(down, hi, 0, cut, EDGE_LOW, chunk_f, across)
        arrived(HIGH, chunk_f, block)
        push(up, hi, half, half, FAR_HIGH, chunk_f, below)
        push(up, hi, 0, cut, EDGE_HIGH, chunk_f, across)

    chunk_s = step - LAG_SECOND

    @pl.when((chunk_s >= 0) & (chunk_s < chunks))
    def _():
        arrived(MIX_LOW, chunk_s, mixed)
        push(down, 1 - hi, cut, mixed // 2, MIXFAR_LOW, chunk_s, above)
        arrived(MIX_HIGH, chunk_s, mixed)
        push(up, 1 - hi, middle, mixed // 2, MIXFAR_HIGH, chunk_s, below)
        arrived(FAR_LOW, chunk_s, half)
        push(far, hi, 0, cut, EDGE_FAR, chunk_s, across)

    @pl.when(step == 0)
    def _():
        pick(2)
        permute(2)
        regroup(2)

    @pl.when(step == 1)
    def _():
        pick(3)
        permute(3)
        regroup(3)
        pick(4)

    @pl.when(step == 2)
    def _():
        permute(4)
        regroup(4)

    @pl.when(step == 3)
    def _():
        permute(5)
        regroup(5)

    @pl.when(step == 4)
    def _():
        permute(6)
        regroup(6)

    @pl.when(step == 5)
    def _():
        permute(7)
        regroup(7)

    @pl.when(step == 1)
    def _():
        w_wait(w_recv_sem, W_ACROSS, 48)
        for d in range(1, 4):
            where = (row, (col + 4 * d) % 16)
            w_send(col, W_ALONG, where)
            w_send(col // 4 * 4 + (col + 2) % 4, W_ALONG, where)

    @pl.when(step == 2)
    def _():
        w_wait(w_recv_sem, W_ALONG, 48 * 6)
        where = (row, col // 2 * 2 + 1 - col % 2)
        for n in range(8):
            w_send(n * 2 + col % 2, W_CORE, where)

    @pl.when(step == LAG_MATMUL)
    def _():
        w_wait(w_recv_sem, W_CORE, 48 * 8)
        size = coupling_t.shape[0]
        high, low = split(coupling_t[...])
        weights[0:size] = high
        weights[size : 2 * size] = low
        weights[2 * size : 3 * size] = high

    chunk_m = step - LAG_MATMUL
    last = out_hbm.shape[0] - (chunks - 1) * width

    def store(chunk, count):
        start = pl.multiple_of(chunk * width, width)
        return pltpu.make_async_copy(
            results.at[chunk % 2, pl.ds(0, count)],
            out_hbm.at[pl.ds(start, count)],
            store_sem.at[chunk % 2],
        )

    @pl.when(chunk_m >= 0)
    def _():
        arrived(FAR_HIGH, chunk_m, half)
        arrived(EDGE_LOW, chunk_m, cut)
        arrived(EDGE_HIGH, chunk_m, cut)
        arrived(EDGE_FAR, chunk_m, cut)
        arrived(MIXFAR_LOW, chunk_m, mixed // 2)
        arrived(MIXFAR_HIGH, chunk_m, mixed // 2)
        size = panel.shape[0]
        high, low = split(panel[:, lanes(chunk_m)].T)
        factors[:, 0:size] = high
        factors[:, size : 2 * size] = high
        factors[:, 2 * size : 3 * size] = low
        slot = chunk_m % 2

        @pl.when(chunk_m >= 2)
        def _():
            store(chunk_m - 2, width).wait()

        results[slot] = residual_ref[...] + jnp.dot(
            factors[...], weights[...], preferred_element_type=F32
        )

        @pl.when(chunk_m < chunks - 1)
        def _():
            store(chunk_m, width).start()

        @pl.when(chunk_m == chunks - 1)
        def _():
            store(chunks - 1, last).start()

    @pl.when(step == pl.num_programs(0) - 1)
    def _():
        store(chunks - 2, width).wait()
        store(chunks - 1, last).wait()
        everything = pl.ds(0, chunks * width)
        ref = incoming.at[pl.ds(0, 15), pl.ds(0, 6), everything]
        pltpu.make_async_copy(ref, ref, send_sem.at[REGROUP]).wait()
        counts = {ACROSS: block, LOW: block, HIGH: block, FAR_LOW: half, FAR_HIGH: half}
        counts |= {MIX_LOW: mixed, MIX_HIGH: mixed, EDGE_LOW: cut, EDGE_HIGH: cut, EDGE_FAR: cut}
        counts |= {MIXFAR_LOW: mixed // 2, MIXFAR_HIGH: mixed // 2}
        for kind, count in counts.items():
            ref = panel.at[pl.ds(0, count), everything]
            pltpu.make_async_copy(ref, ref, send_sem.at[kind]).wait()
        w_wait(w_send_sem, W_ACROSS, 48)
        w_wait(w_send_sem, W_ALONG, 48 * 6)
        w_wait(w_send_sem, W_CORE, 48 * 8)


def shards(residual, cycle_coupling, pair_amps, occupied_order, virtual_order):
    occupied = occupied_order.shape[0]
    virtual = virtual_order.shape[0]
    local_rows, local_columns = residual.shape
    residual = residual.T
    coupling = cycle_coupling.reshape(local_rows, cycle_coupling.shape[2]).T
    depth = local_rows
    chunks = pl.cdiv(local_columns, LANES)
    padded = chunks * LANES
    columns = local_columns // virtual
    steps = chunks + LAG_MATMUL

    def at(step):
        return jnp.maximum(step - LAG_MATMUL, 0), 0

    def whole(shape):
        return pl.BlockSpec(shape, lambda step: (0, 0))

    anywhere = pl.BlockSpec(memory_space=pl.ANY)
    return pl.pallas_call(
        functools.partial(kernel, chunks),
        grid=(steps,),
        out_shape=pltpu.VMEM(residual.shape, F32),
        in_specs=[
            whole((1, occupied)),
            pl.BlockSpec((virtual,), lambda step: (0,)),
            anywhere,
            anywhere,
            pl.BlockSpec((LANES, local_rows), at),
        ],
        out_specs=anywhere,
        scratch_shapes=[
            pltpu.VMEM(pair_amps.shape, F32),
            pltpu.VMEM((2, 6 * occupied, virtual), BF16),
            pltpu.VMEM((columns, 256, virtual), BF16),
            pltpu.VMEM((16, 8, padded), F32),
            pltpu.VMEM((16, 8, padded), F32),
            pltpu.VMEM((depth, padded), F32),
            pltpu.VMEM((depth, local_rows), F32),
            pltpu.VMEM((3 * depth, local_rows), BF16),
            pltpu.VMEM((LANES, 3 * depth), BF16),
            pltpu.VMEM((2, LANES, local_rows), F32),
            pltpu.SemaphoreType.DMA((2,)),
            pltpu.SemaphoreType.DMA((2,)),
            pltpu.SemaphoreType.DMA((KINDS,)),
            pltpu.SemaphoreType.DMA((chunks, KINDS)),
            pltpu.SemaphoreType.DMA((3,)),
            pltpu.SemaphoreType.DMA((3,)),
        ],
        compiler_params=pltpu.CompilerParams(
            collective_id=0, has_side_effects=True, vmem_limit_bytes=48 * 2**20
        ),
        cost_estimate=pl.CostEstimate(
            flops=6 * local_rows * depth * local_columns,
            bytes_accessed=8 * local_rows * local_columns,
            transcendentals=0,
        ),
    )(
        occupied_order.reshape(1, occupied),
        virtual_order,
        pair_amps,
        coupling,
        residual,
    ).T


def solution(mesh):
    in_specs = (P("row", "col"), P("row", None, "col"), P(None, ("row", "col")), P(), P())
    out_specs = P("row", "col")
    return jax.shard_map(shards, mesh=mesh, in_specs=in_specs, out_specs=out_specs, check_vma=False)
```

```python
import functools

import jax
import jax.numpy as jnp
from jax import lax
from jax.experimental import pallas as pl
from jax.experimental.pallas import tpu as pltpu
from jax.sharding import PartitionSpec as P

F32 = jnp.float32
BF16 = jnp.bfloat16
MESH = pl.DeviceIdType.MESH

LANES = 512
LAG_REGROUP = 0
LAG_FIRST = 1
LAG_SECOND = 2
LAG_MATMUL = 3

REGROUP, ACROSS, LOW, HIGH, FAR_LOW, FAR_HIGH, MIX_LOW, MIX_HIGH, MIXFAR_LOW, MIXFAR_HIGH = range(10)
EDGE_LOW, EDGE_HIGH, EDGE_FAR = range(10, 13)
KINDS = 13
GROUPS = {first: 1 for first in range(8)}
W_ACROSS, W_ALONG, W_CORE = range(3)


def split(x):
    high = x.astype(BF16)
    return high, (x - high.astype(F32)).astype(BF16)


def kernel(
    chunks,
    occupied_ref,
    virtual_ref,
    amps_hbm,
    coupling_hbm,
    residual_ref,
    out_hbm,
    amps,
    distance,
    column,
    stored,
    picked,
    outgoing,
    incoming,
    panel,
    coupling_t,
    weights,
    factors,
    results,
    load_sem,
    store_sem,
    send_sem,
    recv_sem,
    w_send_sem,
    w_recv_sem,
):
    step = pl.program_id(0)
    row = lax.axis_index("row")
    col = lax.axis_index("col")
    z, hi = row // 2, row % 2
    up, down, far = (z + 1) % 4, (z + 3) % 4, (z + 2) % 4
    across = (z * 2 + 1 - hi, col)
    above = (up * 2 + hi, col)
    below = (down * 2 + hi, col)
    width = LANES
    block = panel.shape[0] // 8
    blocks, virtual = picked.shape[0], picked.shape[2]
    cut = block // 3
    mixed = block - cut
    half = block // 2
    middle = cut + mixed // 2

    def lanes(chunk):
        return pl.ds(pl.multiple_of(chunk * width, width), width)

    def remote(src, dst, kind, chunk, where):
        pltpu.make_async_remote_copy(
            src_ref=src,
            dst_ref=dst,
            send_sem=send_sem.at[kind],
            recv_sem=recv_sem.at[chunk, kind],
            device_id=where,
            device_id_type=MESH,
        ).start()

    def rows(owner_z, owner_hi, first, count):
        start = (owner_z * 2 + owner_hi) * block + first
        return pl.ds(pl.multiple_of(start, 16), count)

    def push(owner_z, owner_hi, first, count, kind, chunk, where):
        ref = panel.at[rows(owner_z, owner_hi, first, count), lanes(chunk)]
        remote(ref, ref, kind, chunk, where)

    def arrived(kind, chunk, count):
        ref = panel.at[pl.ds(0, count), lanes(chunk)]
        pltpu.make_async_copy(ref, ref, recv_sem.at[chunk, kind]).wait()

    def pick(j):
        one_hot = (distance[...] == j).astype(F32).astype(BF16)
        for s in range(2):
            picked[j, pl.ds(128 * s, 128), :] = jnp.dot(
                one_hot, stored[s], preferred_element_type=F32
            ).astype(BF16)

    def permute(chunk, spanned=2):
        lane = lax.broadcasted_iota(jnp.int32, (virtual, 128), 1)
        first = (chunk * width) // virtual
        total = jnp.zeros((256, width), F32)
        for n in range(spanned):
            j = jnp.minimum(first + n, blocks - 1)
            gap = lane - column[...]
            shift = (first + n) * virtual - chunk * width
            parts = [
                (gap == shift - start).astype(F32).astype(BF16) for start in range(0, width, 128)
            ]
            total += jnp.dot(
                picked[j], jnp.concatenate(parts, axis=1), preferred_element_type=F32
            )
        values = (total[:128] + total[128:]).reshape(16, 8, width)
        outgoing[:, :, lanes(chunk)] = values
        incoming[col, :, lanes(chunk)] = outgoing[col, :, lanes(chunk)]

    def group_lanes(first):
        return pl.ds(first * width, GROUPS[first] * width)

    def regroup(first):
        for d in range(1, 16):
            other = (col + d) % 16
            remote(
                outgoing.at[other, pl.ds(0, 6), group_lanes(first)],
                incoming.at[col, pl.ds(0, 6), group_lanes(first)],
                REGROUP,
                first,
                (row, other),
            )

    def w_wait(sems, kind, count):
        ref = coupling_t.at[pl.ds(0, count)]
        pltpu.make_async_copy(ref, ref, sems.at[kind]).wait()

    def w_send(owner, kind, where):
        ref = coupling_t.at[pl.ds(pl.multiple_of(owner * 48, 16), 48)]
        pltpu.make_async_remote_copy(
            src_ref=ref,
            dst_ref=ref,
            send_sem=w_send_sem.at[kind],
            recv_sem=w_recv_sem.at[kind],
            device_id=where,
            device_id_type=MESH,
        ).start()

    partners = [across, above, below]

    @pl.when(step == 0)
    def _():
        load_amps = pltpu.make_async_copy(amps_hbm, amps, load_sem.at[0])
        load_amps.start()
        own = pl.ds(pl.multiple_of(col * 48, 16), 48)
        load_coupling = pltpu.make_async_copy(coupling_hbm, coupling_t.at[own], load_sem.at[1])
        load_coupling.start()
        barrier = pltpu.get_barrier_semaphore()
        for where in partners:
            pl.semaphore_signal(barrier, inc=1, device_id=where, device_id_type=MESH)
        for d in range(1, 16):
            pl.semaphore_signal(barrier, inc=1, device_id=(row, (col + d) % 16), device_id_type=MESH)
        r = lax.broadcasted_iota(jnp.int32, (128, 480), 0)
        k = lax.broadcasted_iota(jnp.int32, (128, 480), 1)
        order = jnp.concatenate([occupied_ref[...]] * 6, axis=1)
        distance[...] = jnp.where(r % 8 == k // 80, order - (r // 8) * blocks, -1)
        column[...] = jnp.broadcast_to(virtual_ref[...].reshape(1, virtual), (128, virtual)).T
        load_amps.wait()
        for i in range(6):
            high, low = split(amps[:, i * virtual : (i + 1) * virtual])
            stored[0, pl.ds(80 * i, 80), :] = high
            stored[1, pl.ds(80 * i, 80), :] = low
        pick(0)
        permute(0, pl.cdiv(width, virtual))
        pl.semaphore_wait(barrier, 18)
        regroup(0)
        load_coupling.wait()
        w_send(col, W_ACROSS, (row, col // 4 * 4 + (col + 2) % 4))
        pick(1)
        permute(1)
        regroup(1)
        for d in range(1, 4):
            w_send(col, W_ALONG, (row, (col + 4 * d) % 16))

    chunk_r = step - LAG_REGROUP

    @pl.when((chunk_r >= 0) & (chunk_r < chunks))
    def _():
        for first in GROUPS:

            @pl.when(chunk_r == first)
            def _(first=first):
                ref = incoming.at[pl.ds(0, 15), pl.ds(0, 6), group_lanes(first)]
                pltpu.make_async_copy(ref, ref, recv_sem.at[first, REGROUP]).wait()

        pieces = [incoming[q, :, lanes(chunk_r)][:6] for q in range(16)]
        panel[rows(z, hi, 0, block), lanes(chunk_r)] = jnp.concatenate(pieces, axis=0)
        push(z, hi, 0, block, ACROSS, chunk_r, across)
        push(z, hi, 0, block, LOW, chunk_r, above)
        push(z, hi, 0, block, HIGH, chunk_r, below)

    chunk_f = step - LAG_FIRST

    @pl.when((chunk_f >= 0) & (chunk_f < chunks))
    def _():
        arrived(ACROSS, chunk_f, block)
        push(z, 1 - hi, cut, mixed, MIX_LOW, chunk_f, above)
        push(z, 1 - hi, cut, mixed, MIX_HIGH, chunk_f, below)
        arrived(LOW, chunk_f, block)
        push(down, hi, 0, half, FAR_LOW, chunk_f, above)
        push(down, hi, 0, cut, EDGE_LOW, chunk_f, across)
        arrived(HIGH, chunk_f, block)
        push(up, hi, half, half, FAR_HIGH, chunk_f, below)
        push(up, hi, 0, cut, EDGE_HIGH, chunk_f, across)

    chunk_s = step - LAG_SECOND

    @pl.when((chunk_s >= 0) & (chunk_s < chunks))
    def _():
        arrived(MIX_LOW, chunk_s, mixed)
        push(down, 1 - hi, cut, mixed // 2, MIXFAR_LOW, chunk_s, above)
        arrived(MIX_HIGH, chunk_s, mixed)
        push(up, 1 - hi, middle, mixed // 2, MIXFAR_HIGH, chunk_s, below)
        arrived(FAR_LOW, chunk_s, half)
        push(far, hi, 0, cut, EDGE_FAR, chunk_s, across)

    @pl.when(step == 0)
    def _():
        pick(2)
        permute(2)
        regroup(2)

    @pl.when(step == 1)
    def _():
        pick(3)
        permute(3)
        regroup(3)
        pick(4)

    @pl.when(step == 2)
    def _():
        permute(4)
        regroup(4)

    @pl.when(step == 3)
    def _():
        permute(5)
        regroup(5)

    @pl.when(step == 4)
    def _():
        permute(6)
        regroup(6)

    @pl.when(step == 5)
    def _():
        permute(7)
        regroup(7)

    @pl.when(step == 0)
    def _():
        w_wait(w_recv_sem, W_ACROSS, 48)
        for d in range(1, 4):
            w_send(col // 4 * 4 + (col + 2) % 4, W_ALONG, (row, (col + 4 * d) % 16))

    @pl.when(step == LAG_MATMUL)
    def _():
        w_wait(w_recv_sem, W_ALONG, 48 * 6)
        where = (row, col // 2 * 2 + 1 - col % 2)
        for n in range(8):
            w_send(n * 2 + col % 2, W_CORE, where)

    @pl.when(step == LAG_MATMUL)
    def _():
        w_wait(w_recv_sem, W_CORE, 48 * 8)
        size = coupling_t.shape[0]
        high, low = split(coupling_t[...])
        weights[0:size] = high
        weights[size : 2 * size] = low
        weights[2 * size : 3 * size] = high

    chunk_m = step - LAG_MATMUL
    last = out_hbm.shape[0] - (chunks - 1) * width

    def store(chunk, count):
        start = pl.multiple_of(chunk * width, width)
        return pltpu.make_async_copy(
            results.at[chunk % 2, pl.ds(0, count)],
            out_hbm.at[pl.ds(start, count)],
            store_sem.at[chunk % 2],
        )

    @pl.when(chunk_m >= 0)
    def _():
        arrived(FAR_HIGH, chunk_m, half)
        arrived(EDGE_LOW, chunk_m, cut)
        arrived(EDGE_HIGH, chunk_m, cut)
        arrived(EDGE_FAR, chunk_m, cut)
        arrived(MIXFAR_LOW, chunk_m, mixed // 2)
        arrived(MIXFAR_HIGH, chunk_m, mixed // 2)
        size = panel.shape[0]
        high, low = split(panel[:, lanes(chunk_m)].T)
        factors[:, 0:size] = high
        factors[:, size : 2 * size] = high
        factors[:, 2 * size : 3 * size] = low
        slot = chunk_m % 2

        @pl.when(chunk_m >= 2)
        def _():
            store(chunk_m - 2, width).wait()

        results[slot] = residual_ref[...] + jnp.dot(
            factors[...], weights[...], preferred_element_type=F32
        )

        @pl.when(chunk_m < chunks - 1)
        def _():
            store(chunk_m, width).start()

        @pl.when(chunk_m == chunks - 1)
        def _():
            store(chunks - 1, last).start()

    @pl.when(step == pl.num_programs(0) - 1)
    def _():
        store(chunks - 2, width).wait()
        store(chunks - 1, last).wait()
        everything = pl.ds(0, chunks * width)
        ref = incoming.at[pl.ds(0, 15), pl.ds(0, 6), everything]
        pltpu.make_async_copy(ref, ref, send_sem.at[REGROUP]).wait()
        counts = {ACROSS: block, LOW: block, HIGH: block, FAR_LOW: half, FAR_HIGH: half}
        counts |= {MIX_LOW: mixed, MIX_HIGH: mixed, EDGE_LOW: cut, EDGE_HIGH: cut, EDGE_FAR: cut}
        counts |= {MIXFAR_LOW: mixed // 2, MIXFAR_HIGH: mixed // 2}
        for kind, count in counts.items():
            ref = panel.at[pl.ds(0, count), everything]
            pltpu.make_async_copy(ref, ref, send_sem.at[kind]).wait()
        w_wait(w_send_sem, W_ACROSS, 48)
        w_wait(w_send_sem, W_ALONG, 48 * 6)
        w_wait(w_send_sem, W_CORE, 48 * 8)


def shards(residual, cycle_coupling, pair_amps, occupied_order, virtual_order):
    occupied = occupied_order.shape[0]
    virtual = virtual_order.shape[0]
    local_rows, local_columns = residual.shape
    residual = residual.T
    coupling = cycle_coupling.reshape(local_rows, cycle_coupling.shape[2]).T
    depth = local_rows
    chunks = pl.cdiv(local_columns, LANES)
    padded = chunks * LANES
    columns = local_columns // virtual
    steps = chunks + LAG_MATMUL

    def at(step):
        return jnp.maximum(step - LAG_MATMUL, 0), 0

    def whole(shape):
        return pl.BlockSpec(shape, lambda step: (0, 0))

    anywhere = pl.BlockSpec(memory_space=pl.ANY)
    return pl.pallas_call(
        functools.partial(kernel, chunks),
        grid=(steps,),
        out_shape=pltpu.VMEM(residual.shape, F32),
        in_specs=[
            whole((1, occupied)),
            pl.BlockSpec((virtual,), lambda step: (0,)),
            anywhere,
            anywhere,
            pl.BlockSpec((LANES, local_rows), at),
        ],
        out_specs=anywhere,
        scratch_shapes=[
            pltpu.VMEM(pair_amps.shape, F32),
            pltpu.VMEM((128, 6 * occupied), jnp.int32),
            pltpu.VMEM((virtual, 128), jnp.int32),
            pltpu.VMEM((2, 6 * occupied, virtual), BF16),
            pltpu.VMEM((columns, 256, virtual), BF16),
            pltpu.VMEM((16, 8, padded), F32),
            pltpu.VMEM((16, 8, padded), F32),
            pltpu.VMEM((depth, padded), F32),
            pltpu.VMEM((depth, local_rows), F32),
            pltpu.VMEM((3 * depth, local_rows), BF16),
            pltpu.VMEM((LANES, 3 * depth), BF16),
            pltpu.VMEM((2, LANES, local_rows), F32),
            pltpu.SemaphoreType.DMA((2,)),
            pltpu.SemaphoreType.DMA((2,)),
            pltpu.SemaphoreType.DMA((KINDS,)),
            pltpu.SemaphoreType.DMA((chunks, KINDS)),
            pltpu.SemaphoreType.DMA((3,)),
            pltpu.SemaphoreType.DMA((3,)),
        ],
        compiler_params=pltpu.CompilerParams(
            collective_id=0, has_side_effects=True, vmem_limit_bytes=48 * 2**20
        ),
        cost_estimate=pl.CostEstimate(
            flops=6 * local_rows * depth * local_columns,
            bytes_accessed=8 * local_rows * local_columns,
            transcendentals=0,
        ),
    )(
        occupied_order.reshape(1, occupied),
        virtual_order,
        pair_amps,
        coupling,
        residual,
    ).T


def solution(mesh):
    in_specs = (P("row", "col"), P("row", None, "col"), P(None, ("row", "col")), P(), P())
    out_specs = P("row", "col")
    return jax.shard_map(shards, mesh=mesh, in_specs=in_specs, out_specs=out_specs, check_vma=False)
```

```python
import functools

import jax
import jax.numpy as jnp
from jax import lax
from jax.experimental import pallas as pl
from jax.experimental.pallas import tpu as pltpu
from jax.sharding import PartitionSpec as P

F32 = jnp.float32
BF16 = jnp.bfloat16
MESH = pl.DeviceIdType.MESH

LANES = 512
LAG_REGROUP = 0
CUT_EVEN = 32
CUT_ODD = 40
LAG_FIRST = 1
LAG_SECOND = 2
LAG_MATMUL = 3

REGROUP, ACROSS, LOW, HIGH, FAR_LOW, FAR_HIGH, MIX_LOW, MIX_HIGH, MIXFAR_LOW, MIXFAR_HIGH = range(10)
EDGE_LOW, EDGE_HIGH, EDGE_FAR = range(10, 13)
KINDS = 13
GROUPS = {first: 1 for first in range(8)}
W_ACROSS, W_ALONG, W_CORE = range(3)


def split(x):
    high = x.astype(BF16)
    return high, (x - high.astype(F32)).astype(BF16)


def kernel(
    chunks,
    occupied_ref,
    virtual_ref,
    amps_hbm,
    coupling_hbm,
    residual_ref,
    out_hbm,
    amps,
    distance,
    column,
    stored,
    picked,
    outgoing,
    incoming,
    panel,
    coupling_t,
    weights,
    factors,
    results,
    load_sem,
    store_sem,
    send_sem,
    recv_sem,
    w_send_sem,
    w_recv_sem,
):
    step = pl.program_id(0)
    row = lax.axis_index("row")
    col = lax.axis_index("col")
    z, hi = row // 2, row % 2
    up, down, far = (z + 1) % 4, (z + 3) % 4, (z + 2) % 4
    lo = col // 2 % 2

    def swapped_from(parity):
        return (lo + parity) % 2

    across = (z * 2 + 1 - hi, col)
    above = (up * 2 + hi, col)
    below = (down * 2 + hi, col)
    width = LANES
    block = panel.shape[0] // 8
    blocks, virtual = picked.shape[0], picked.shape[2]
    half = block // 2
    cuts = (CUT_EVEN, CUT_ODD)
    lows = tuple(pl.cdiv(block - cut, 16) * 8 for cut in cuts)

    def lanes(chunk):
        return pl.ds(pl.multiple_of(chunk * width, width), width)

    def remote(src, dst, kind, chunk, where):
        pltpu.make_async_remote_copy(
            src_ref=src,
            dst_ref=dst,
            send_sem=send_sem.at[kind],
            recv_sem=recv_sem.at[chunk, kind],
            device_id=where,
            device_id_type=MESH,
        ).start()

    def rows(owner_z, owner_hi, first, count):
        start = (owner_z * 2 + owner_hi) * block + first
        return pl.ds(pl.multiple_of(start, 8), count)

    def push(owner_z, owner_hi, first, count, kind, chunk, where):
        ref = panel.at[rows(owner_z, owner_hi, first, count), lanes(chunk)]
        remote(ref, ref, kind, chunk, where)

    def arrived(kind, chunk, count):
        ref = panel.at[pl.ds(0, count), lanes(chunk)]
        pltpu.make_async_copy(ref, ref, recv_sem.at[chunk, kind]).wait()

    def pick(j):
        one_hot = (distance[...] == j).astype(F32).astype(BF16)
        for s in range(2):
            picked[j, pl.ds(128 * s, 128), :] = jnp.dot(
                one_hot, stored[s], preferred_element_type=F32
            ).astype(BF16)

    def permute(chunk, spanned=2):
        lane = lax.broadcasted_iota(jnp.int32, (virtual, 128), 1)
        first = (chunk * width) // virtual
        total = jnp.zeros((256, width), F32)
        for n in range(spanned):
            j = jnp.minimum(first + n, blocks - 1)
            gap = lane - column[...]
            shift = (first + n) * virtual - chunk * width
            parts = [
                (gap == shift - start).astype(F32).astype(BF16) for start in range(0, width, 128)
            ]
            total += jnp.dot(
                picked[j], jnp.concatenate(parts, axis=1), preferred_element_type=F32
            )
        values = (total[:128] + total[128:]).reshape(16, 8, width)
        outgoing[:, :, lanes(chunk)] = values
        incoming[col, :, lanes(chunk)] = outgoing[col, :, lanes(chunk)]

    def group_lanes(first):
        return pl.ds(first * width, GROUPS[first] * width)

    def regroup(first):
        for d in range(1, 16):
            other = (col + d) % 16
            crossed = ((other // 2 % 2 != lo) & (swapped_from(first % 2) == 1)).astype(jnp.int32)
            remote(
                outgoing.at[other, pl.ds(0, 6), group_lanes(first)],
                incoming.at[col, pl.ds(0, 6), group_lanes(first)],
                REGROUP,
                first,
                (z * 2 + (hi + crossed) % 2, other),
            )

    def w_wait(sems, kind, count):
        ref = coupling_t.at[pl.ds(0, count)]
        pltpu.make_async_copy(ref, ref, sems.at[kind]).wait()

    def w_send(owner, kind, where):
        ref = coupling_t.at[pl.ds(pl.multiple_of(owner * 48, 16), 48)]
        pltpu.make_async_remote_copy(
            src_ref=ref,
            dst_ref=ref,
            send_sem=w_send_sem.at[kind],
            recv_sem=w_recv_sem.at[kind],
            device_id=where,
            device_id_type=MESH,
        ).start()

    partners = [across, above, below]

    @pl.when(step == 0)
    def _():
        load_amps = pltpu.make_async_copy(amps_hbm, amps, load_sem.at[0])
        load_amps.start()
        own = pl.ds(pl.multiple_of(col * 48, 16), 48)
        load_coupling = pltpu.make_async_copy(coupling_hbm, coupling_t.at[own], load_sem.at[1])
        load_coupling.start()
        barrier = pltpu.get_barrier_semaphore()
        for where in partners:
            pl.semaphore_signal(barrier, inc=1, device_id=where, device_id_type=MESH)
        for d in range(1, 16):
            pl.semaphore_signal(barrier, inc=1, device_id=(row, (col + d) % 16), device_id_type=MESH)
        for n in range(8):
            other = n // 2 * 4 + (1 - lo) * 2 + n % 2
            pl.semaphore_signal(barrier, inc=1, device_id=(across[0], other), device_id_type=MESH)
        r = lax.broadcasted_iota(jnp.int32, (128, 480), 0)
        k = lax.broadcasted_iota(jnp.int32, (128, 480), 1)
        order = jnp.concatenate([occupied_ref[...]] * 6, axis=1)
        distance[...] = jnp.where(r % 8 == k // 80, order - (r // 8) * blocks, -1)
        column[...] = jnp.broadcast_to(virtual_ref[...].reshape(1, virtual), (128, virtual)).T
        load_amps.wait()
        for i in range(6):
            high, low = split(amps[:, i * virtual : (i + 1) * virtual])
            stored[0, pl.ds(80 * i, 80), :] = high
            stored[1, pl.ds(80 * i, 80), :] = low
        pick(0)
        permute(0, pl.cdiv(width, virtual))
        pl.semaphore_wait(barrier, 26)
        regroup(0)
        load_coupling.wait()
        w_send(col, W_ACROSS, (row, col // 4 * 4 + (col + 2) % 4))
        pick(1)
        permute(1)
        regroup(1)
        for d in range(1, 4):
            w_send(col, W_ALONG, (row, (col + 4 * d) % 16))

    chunk_r = step - LAG_REGROUP

    @pl.when((chunk_r >= 0) & (chunk_r < chunks))
    def _():
        for first in GROUPS:

            @pl.when(chunk_r == first)
            def _(first=first):
                ref = incoming.at[pl.ds(0, 15), pl.ds(0, 6), group_lanes(first)]
                pltpu.make_async_copy(ref, ref, recv_sem.at[first, REGROUP]).wait()

        pieces = [incoming[q, :, lanes(chunk_r)][:6] for q in range(16)]
        panel[rows(z, hi, 0, block), lanes(chunk_r)] = jnp.concatenate(pieces, axis=0)
        push(z, hi, 0, block, ACROSS, chunk_r, across)
        push(z, hi, 0, block, LOW, chunk_r, above)
        push(z, hi, 0, block, HIGH, chunk_r, below)

    def first_stage(chunk, cut, low):
        arrived(ACROSS, chunk, block)
        push(z, 1 - hi, cut, block - cut, MIX_LOW, chunk, above)
        push(z, 1 - hi, cut, block - cut, MIX_HIGH, chunk, below)
        arrived(LOW, chunk, block)
        push(down, hi, 0, half, FAR_LOW, chunk, above)
        push(down, hi, 0, cut, EDGE_LOW, chunk, across)
        arrived(HIGH, chunk, block)
        push(up, hi, half, half, FAR_HIGH, chunk, below)
        push(up, hi, 0, cut, EDGE_HIGH, chunk, across)

    def second_stage(chunk, cut, low):
        arrived(MIX_LOW, chunk, block - cut)
        push(down, 1 - hi, cut, low, MIXFAR_LOW, chunk, above)
        arrived(MIX_HIGH, chunk, block - cut)
        push(up, 1 - hi, cut + low, block - cut - low, MIXFAR_HIGH, chunk, below)
        arrived(FAR_LOW, chunk, half)
        push(far, hi, 0, cut, EDGE_FAR, chunk, across)

    def last_stage(chunk, cut, low):
        arrived(FAR_HIGH, chunk, half)
        arrived(EDGE_LOW, chunk, cut)
        arrived(EDGE_HIGH, chunk, cut)
        arrived(EDGE_FAR, chunk, cut)
        arrived(MIXFAR_LOW, chunk, low)
        arrived(MIXFAR_HIGH, chunk, block - cut - low)

    def by_parity(stage, chunk):
        for parity in range(2):

            @pl.when((chunk >= 0) & (chunk < chunks) & (chunk % 2 == parity))
            def _(parity=parity):
                stage(chunk, cuts[parity], lows[parity])

    by_parity(first_stage, step - LAG_FIRST)
    by_parity(second_stage, step - LAG_SECOND)

    @pl.when(step == 0)
    def _():
        pick(2)
        permute(2)
        regroup(2)

    @pl.when(step == 1)
    def _():
        pick(3)
        permute(3)
        regroup(3)
        pick(4)

    @pl.when(step == 2)
    def _():
        permute(4)
        regroup(4)

    @pl.when(step == 3)
    def _():
        permute(5)
        regroup(5)

    @pl.when(step == 4)
    def _():
        permute(6)
        regroup(6)

    @pl.when(step == 5)
    def _():
        permute(7)
        regroup(7)

    @pl.when(step == 0)
    def _():
        w_wait(w_recv_sem, W_ACROSS, 48)
        for d in range(1, 4):
            w_send(col // 4 * 4 + (col + 2) % 4, W_ALONG, (row, (col + 4 * d) % 16))

    @pl.when(step == LAG_MATMUL)
    def _():
        w_wait(w_recv_sem, W_ALONG, 48 * 6)
        where = (row, col // 2 * 2 + 1 - col % 2)
        for n in range(8):
            w_send(n * 2 + col % 2, W_CORE, where)

    @pl.when(step == LAG_MATMUL)
    def _():
        w_wait(w_recv_sem, W_CORE, 48 * 8)
        size = coupling_t.shape[0]
        r = lax.broadcasted_iota(jnp.int32, (block, 1), 0)
        crossing = r // 12 % 2 != lo
        for parity in range(2):
            swap = crossing & ((lo + parity) % 2 == 0)
            for n in range(8):
                mine = coupling_t[n * block : (n + 1) * block]
                twin = coupling_t[(n ^ 1) * block : (n ^ 1) * block + block]
                high, low = split(jnp.where(swap, twin, mine))
                weights[parity, n * block : (n + 1) * block] = high
                weights[parity, size + n * block : size + (n + 1) * block] = low
                weights[parity, 2 * size + n * block : 2 * size + (n + 1) * block] = high

    chunk_m = step - LAG_MATMUL
    last = out_hbm.shape[0] - (chunks - 1) * width

    def store(chunk, count):
        start = pl.multiple_of(chunk * width, width)
        return pltpu.make_async_copy(
            results.at[chunk % 2, pl.ds(0, count)],
            out_hbm.at[pl.ds(start, count)],
            store_sem.at[chunk % 2],
        )

    by_parity(last_stage, chunk_m)

    @pl.when(chunk_m >= 0)
    def _():
        size = panel.shape[0]
        high, low = split(panel[:, lanes(chunk_m)].T)
        factors[:, 0:size] = high
        factors[:, size : 2 * size] = high
        factors[:, 2 * size : 3 * size] = low
        slot = chunk_m % 2

        @pl.when(chunk_m >= 2)
        def _():
            store(chunk_m - 2, width).wait()

        results[slot] = residual_ref[...] + jnp.dot(
            factors[...], weights[slot], preferred_element_type=F32
        )

        @pl.when(chunk_m < chunks - 1)
        def _():
            store(chunk_m, width).start()

        @pl.when(chunk_m == chunks - 1)
        def _():
            store(chunks - 1, last).start()

    @pl.when(step == pl.num_programs(0) - 1)
    def _():
        store(chunks - 2, width).wait()
        store(chunks - 1, last).wait()
        everything = pl.ds(0, chunks * width)
        ref = incoming.at[pl.ds(0, 15), pl.ds(0, 6), everything]
        pltpu.make_async_copy(ref, ref, send_sem.at[REGROUP]).wait()
        edge, low = sum(cuts), sum(lows)
        counts = {ACROSS: 2 * block, LOW: 2 * block, HIGH: 2 * block}
        counts |= {FAR_LOW: 2 * half, FAR_HIGH: 2 * half}
        counts |= {EDGE_LOW: edge, EDGE_HIGH: edge, EDGE_FAR: edge}
        counts |= {MIX_LOW: 2 * block - edge, MIX_HIGH: 2 * block - edge}
        counts |= {MIXFAR_LOW: low, MIXFAR_HIGH: 2 * block - edge - low}
        for kind, count in counts.items():
            ref = panel.at[pl.ds(0, count), pl.ds(0, chunks // 2 * width)]
            pltpu.make_async_copy(ref, ref, send_sem.at[kind]).wait()
        w_wait(w_send_sem, W_ACROSS, 48)
        w_wait(w_send_sem, W_ALONG, 48 * 6)
        w_wait(w_send_sem, W_CORE, 48 * 8)


def shards(residual, cycle_coupling, pair_amps, occupied_order, virtual_order):
    occupied = occupied_order.shape[0]
    virtual = virtual_order.shape[0]
    local_rows, local_columns = residual.shape
    residual = residual.T
    coupling = cycle_coupling.reshape(local_rows, cycle_coupling.shape[2]).T
    depth = local_rows
    chunks = pl.cdiv(local_columns, LANES)
    padded = chunks * LANES
    columns = local_columns // virtual
    steps = chunks + LAG_MATMUL

    def at(step):
        return jnp.maximum(step - LAG_MATMUL, 0), 0

    def whole(shape):
        return pl.BlockSpec(shape, lambda step: (0, 0))

    anywhere = pl.BlockSpec(memory_space=pl.ANY)
    return pl.pallas_call(
        functools.partial(kernel, chunks),
        grid=(steps,),
        out_shape=pltpu.VMEM(residual.shape, F32),
        in_specs=[
            whole((1, occupied)),
            pl.BlockSpec((virtual,), lambda step: (0,)),
            anywhere,
            anywhere,
            pl.BlockSpec((LANES, local_rows), at),
        ],
        out_specs=anywhere,
        scratch_shapes=[
            pltpu.VMEM(pair_amps.shape, F32),
            pltpu.VMEM((128, 6 * occupied), jnp.int32),
            pltpu.VMEM((virtual, 128), jnp.int32),
            pltpu.VMEM((2, 6 * occupied, virtual), BF16),
            pltpu.VMEM((columns, 256, virtual), BF16),
            pltpu.VMEM((16, 8, padded), F32),
            pltpu.VMEM((16, 8, padded), F32),
            pltpu.VMEM((depth, padded), F32),
            pltpu.VMEM((depth, local_rows), F32),
            pltpu.VMEM((2, 3 * depth, local_rows), BF16),
            pltpu.VMEM((LANES, 3 * depth), BF16),
            pltpu.VMEM((2, LANES, local_rows), F32),
            pltpu.SemaphoreType.DMA((2,)),
            pltpu.SemaphoreType.DMA((2,)),
            pltpu.SemaphoreType.DMA((KINDS,)),
            pltpu.SemaphoreType.DMA((chunks, KINDS)),
            pltpu.SemaphoreType.DMA((3,)),
            pltpu.SemaphoreType.DMA((3,)),
        ],
        compiler_params=pltpu.CompilerParams(
            collective_id=0, has_side_effects=True, vmem_limit_bytes=48 * 2**20
        ),
        cost_estimate=pl.CostEstimate(
            flops=6 * local_rows * depth * local_columns,
            bytes_accessed=8 * local_rows * local_columns,
            transcendentals=0,
        ),
    )(
        occupied_order.reshape(1, occupied),
        virtual_order,
        pair_amps,
        coupling,
        residual,
    ).T


def solution(mesh):
    in_specs = (P("row", "col"), P("row", None, "col"), P(None, ("row", "col")), P(), P())
    out_specs = P("row", "col")
    return jax.shard_map(shards, mesh=mesh, in_specs=in_specs, out_specs=out_specs, check_vma=False)
```

```python
import functools

import jax
import jax.numpy as jnp
from jax import lax
from jax.experimental import pallas as pl
from jax.experimental.pallas import tpu as pltpu
from jax.sharding import PartitionSpec as P

F32 = jnp.float32
BF16 = jnp.bfloat16
MESH = pl.DeviceIdType.MESH

LANES = 512
LAG_REGROUP = 0
CUT_EVEN = 40
CUT_ODD = 40
LAG_FIRST = 1
LAG_SECOND = 2
LAG_MATMUL = 3

REGROUP, ACROSS, LOW, HIGH, FAR_LOW, FAR_HIGH, MIX_LOW, MIX_HIGH, MIXFAR_LOW, MIXFAR_HIGH = range(10)
EDGE_LOW, EDGE_HIGH, EDGE_FAR = range(10, 13)
KINDS = 13
GROUPS = {first: 1 for first in range(8)}
W_ACROSS, W_ALONG, W_CORE = range(3)


def split(x):
    high = x.astype(BF16)
    return high, (x - high.astype(F32)).astype(BF16)


def kernel(
    chunks,
    occupied_ref,
    virtual_ref,
    amps_hbm,
    coupling_hbm,
    residual_ref,
    out_hbm,
    amps,
    distance,
    column,
    stored,
    picked,
    outgoing,
    incoming,
    panel,
    coupling_t,
    weights,
    factors,
    results,
    load_sem,
    store_sem,
    send_sem,
    recv_sem,
    w_send_sem,
    w_recv_sem,
):
    step = pl.program_id(0)
    row = lax.axis_index("row")
    col = lax.axis_index("col")
    z, hi = row // 2, row % 2
    up, down, far = (z + 1) % 4, (z + 3) % 4, (z + 2) % 4
    lo = col // 2 % 2

    def swapped_from(parity):
        return (lo + parity) % 2

    across = (z * 2 + 1 - hi, col)
    above = (up * 2 + hi, col)
    below = (down * 2 + hi, col)
    width = LANES
    block = panel.shape[0] // 8
    blocks, virtual = picked.shape[0], picked.shape[2]
    half = block // 2
    cuts = (CUT_EVEN, CUT_ODD)
    lows = tuple(pl.cdiv(block - cut, 16) * 8 for cut in cuts)

    def lanes(chunk):
        return pl.ds(pl.multiple_of(chunk * width, width), width)

    def remote(src, dst, kind, chunk, where):
        pltpu.make_async_remote_copy(
            src_ref=src,
            dst_ref=dst,
            send_sem=send_sem.at[kind],
            recv_sem=recv_sem.at[chunk, kind],
            device_id=where,
            device_id_type=MESH,
        ).start()

    def rows(owner_z, owner_hi, first, count):
        start = (owner_z * 2 + owner_hi) * block + first
        return pl.ds(pl.multiple_of(start, 8), count)

    def push(owner_z, owner_hi, first, count, kind, chunk, where):
        ref = panel.at[rows(owner_z, owner_hi, first, count), lanes(chunk)]
        remote(ref, ref, kind, chunk, where)

    def arrived(kind, chunk, count):
        ref = panel.at[pl.ds(0, count), lanes(chunk)]
        pltpu.make_async_copy(ref, ref, recv_sem.at[chunk, kind]).wait()

    def pick(j):
        one_hot = (distance[...] == j).astype(F32).astype(BF16)
        for s in range(2):
            picked[j, pl.ds(128 * s, 128), :] = jnp.dot(
                one_hot, stored[s], preferred_element_type=F32
            ).astype(BF16)

    def permute(chunk, spanned=2):
        lane = lax.broadcasted_iota(jnp.int32, (virtual, 128), 1)
        first = (chunk * width) // virtual
        total = jnp.zeros((256, width), F32)
        for n in range(spanned):
            j = jnp.minimum(first + n, blocks - 1)
            gap = lane - column[...]
            shift = (first + n) * virtual - chunk * width
            parts = [
                (gap == shift - start).astype(F32).astype(BF16) for start in range(0, width, 128)
            ]
            total += jnp.dot(
                picked[j], jnp.concatenate(parts, axis=1), preferred_element_type=F32
            )
        values = (total[:128] + total[128:]).reshape(16, 8, width)
        outgoing[:, :, lanes(chunk)] = values
        incoming[col, :, lanes(chunk)] = outgoing[col, :, lanes(chunk)]

    def group_lanes(first):
        return pl.ds(first * width, GROUPS[first] * width)

    def regroup(first):
        for d in range(1, 16):
            other = (col + d) % 16
            crossed = ((other // 2 % 2 != lo) & (swapped_from(first % 2) == 1)).astype(jnp.int32)
            remote(
                outgoing.at[other, pl.ds(0, 6), group_lanes(first)],
                incoming.at[col, pl.ds(0, 6), group_lanes(first)],
                REGROUP,
                first,
                (z * 2 + (hi + crossed) % 2, other),
            )

    def w_wait(sems, kind, count):
        ref = coupling_t.at[pl.ds(0, count)]
        pltpu.make_async_copy(ref, ref, sems.at[kind]).wait()

    def w_send(owner, kind, where):
        ref = coupling_t.at[pl.ds(pl.multiple_of(owner * 48, 16), 48)]
        pltpu.make_async_remote_copy(
            src_ref=ref,
            dst_ref=ref,
            send_sem=w_send_sem.at[kind],
            recv_sem=w_recv_sem.at[kind],
            device_id=where,
            device_id_type=MESH,
        ).start()

    partners = [across, above, below]

    @pl.when(step == 0)
    def _():
        load_amps = pltpu.make_async_copy(amps_hbm, amps, load_sem.at[0])
        load_amps.start()
        own = pl.ds(pl.multiple_of(col * 48, 16), 48)
        load_coupling = pltpu.make_async_copy(coupling_hbm, coupling_t.at[own], load_sem.at[1])
        load_coupling.start()
        barrier = pltpu.get_barrier_semaphore()
        for where in partners:
            pl.semaphore_signal(barrier, inc=1, device_id=where, device_id_type=MESH)
        for d in range(1, 16):
            pl.semaphore_signal(barrier, inc=1, device_id=(row, (col + d) % 16), device_id_type=MESH)
        for n in range(8):
            other = n // 2 * 4 + (1 - lo) * 2 + n % 2
            pl.semaphore_signal(barrier, inc=1, device_id=(across[0], other), device_id_type=MESH)
        r = lax.broadcasted_iota(jnp.int32, (128, 480), 0)
        k = lax.broadcasted_iota(jnp.int32, (128, 480), 1)
        order = jnp.concatenate([occupied_ref[...]] * 6, axis=1)
        distance[...] = jnp.where(r % 8 == k // 80, order - (r // 8) * blocks, -1)
        column[...] = jnp.broadcast_to(virtual_ref[...].reshape(1, virtual), (128, virtual)).T
        load_amps.wait()
        for i in range(6):
            high, low = split(amps[:, i * virtual : (i + 1) * virtual])
            stored[0, pl.ds(80 * i, 80), :] = high
            stored[1, pl.ds(80 * i, 80), :] = low
        pick(0)
        permute(0, pl.cdiv(width, virtual))
        pl.semaphore_wait(barrier, 26)
        regroup(0)
        load_coupling.wait()
        w_send(col, W_ACROSS, (row, col // 4 * 4 + (col + 2) % 4))
        pick(1)
        permute(1)
        regroup(1)
        for d in range(1, 4):
            w_send(col, W_ALONG, (row, (col + 4 * d) % 16))

    chunk_r = step - LAG_REGROUP

    @pl.when((chunk_r >= 0) & (chunk_r < chunks))
    def _():
        for first in GROUPS:

            @pl.when(chunk_r == first)
            def _(first=first):
                ref = incoming.at[pl.ds(0, 15), pl.ds(0, 6), group_lanes(first)]
                pltpu.make_async_copy(ref, ref, recv_sem.at[first, REGROUP]).wait()

        pieces = [incoming[q, :, lanes(chunk_r)][:6] for q in range(16)]
        panel[rows(z, hi, 0, block), lanes(chunk_r)] = jnp.concatenate(pieces, axis=0)
        push(z, hi, 0, block, ACROSS, chunk_r, across)
        push(z, hi, 0, block, LOW, chunk_r, above)
        push(z, hi, 0, block, HIGH, chunk_r, below)

    def first_stage(chunk, cut, low):
        arrived(ACROSS, chunk, block)
        push(z, 1 - hi, cut, block - cut, MIX_LOW, chunk, above)
        push(z, 1 - hi, cut, block - cut, MIX_HIGH, chunk, below)
        arrived(LOW, chunk, block)
        push(down, hi, 0, half, FAR_LOW, chunk, above)
        push(down, hi, 0, cut, EDGE_LOW, chunk, across)
        arrived(HIGH, chunk, block)
        push(up, hi, half, half, FAR_HIGH, chunk, below)
        push(up, hi, 0, cut, EDGE_HIGH, chunk, across)

    def second_stage(chunk, cut, low):
        arrived(MIX_LOW, chunk, block - cut)
        push(down, 1 - hi, cut, low, MIXFAR_LOW, chunk, above)
        arrived(MIX_HIGH, chunk, block - cut)
        push(up, 1 - hi, cut + low, block - cut - low, MIXFAR_HIGH, chunk, below)
        arrived(FAR_LOW, chunk, half)
        push(far, hi, 0, cut, EDGE_FAR, chunk, across)

    def last_stage(chunk, cut, low):
        arrived(FAR_HIGH, chunk, half)
        arrived(EDGE_LOW, chunk, cut)
        arrived(EDGE_HIGH, chunk, cut)
        arrived(EDGE_FAR, chunk, cut)
        arrived(MIXFAR_LOW, chunk, low)
        arrived(MIXFAR_HIGH, chunk, block - cut - low)

    def by_parity(stage, chunk):
        for parity in range(2):

            @pl.when((chunk >= 0) & (chunk < chunks) & (chunk % 2 == parity))
            def _(parity=parity):
                stage(chunk, cuts[parity], lows[parity])

    by_parity(first_stage, step - LAG_FIRST)
    by_parity(second_stage, step - LAG_SECOND)

    @pl.when(step == 0)
    def _():
        pick(2)
        permute(2)
        regroup(2)

    @pl.when(step == 1)
    def _():
        pick(3)
        permute(3)
        regroup(3)
        pick(4)

    @pl.when(step == 2)
    def _():
        permute(4)
        regroup(4)

    @pl.when(step == 3)
    def _():
        permute(5)
        regroup(5)

    @pl.when(step == 4)
    def _():
        permute(6)
        regroup(6)

    @pl.when(step == 5)
    def _():
        permute(7)
        regroup(7)

    @pl.when(step == 0)
    def _():
        w_wait(w_recv_sem, W_ACROSS, 48)
        for d in range(1, 4):
            w_send(col // 4 * 4 + (col + 2) % 4, W_ALONG, (row, (col + 4 * d) % 16))

    @pl.when(step == LAG_MATMUL)
    def _():
        w_wait(w_recv_sem, W_ALONG, 48 * 6)
        where = (row, col // 2 * 2 + 1 - col % 2)
        for n in range(8):
            w_send(n * 2 + col % 2, W_CORE, where)

    @pl.when(step == LAG_MATMUL)
    def _():
        w_wait(w_recv_sem, W_CORE, 48 * 8)
        size = coupling_t.shape[0]
        r = lax.broadcasted_iota(jnp.int32, (block, 1), 0)
        crossing = r // 12 % 2 != lo
        for parity in range(2):
            swap = crossing & ((lo + parity) % 2 == 0)
            for n in range(8):
                mine = coupling_t[n * block : (n + 1) * block]
                twin = coupling_t[(n ^ 1) * block : (n ^ 1) * block + block]
                high, low = split(jnp.where(swap, twin, mine))
                weights[parity, n * block : (n + 1) * block] = high
                weights[parity, size + n * block : size + (n + 1) * block] = low
                weights[parity, 2 * size + n * block : 2 * size + (n + 1) * block] = high

    chunk_m = step - LAG_MATMUL
    last = out_hbm.shape[0] - (chunks - 1) * width

    def store(chunk, count):
        start = pl.multiple_of(chunk * width, width)
        return pltpu.make_async_copy(
            results.at[chunk % 2, pl.ds(0, count)],
            out_hbm.at[pl.ds(start, count)],
            store_sem.at[chunk % 2],
        )

    by_parity(last_stage, chunk_m)

    @pl.when(chunk_m >= 0)
    def _():
        size = panel.shape[0]
        high, low = split(panel[:, lanes(chunk_m)].T)
        factors[:, 0:size] = high
        factors[:, size : 2 * size] = high
        factors[:, 2 * size : 3 * size] = low
        slot = chunk_m % 2

        @pl.when(chunk_m >= 2)
        def _():
            store(chunk_m - 2, width).wait()

        results[slot] = residual_ref[...] + jnp.dot(
            factors[...], weights[slot], preferred_element_type=F32
        )

        @pl.when(chunk_m < chunks - 1)
        def _():
            store(chunk_m, width).start()

        @pl.when(chunk_m == chunks - 1)
        def _():
            store(chunks - 1, last).start()

    @pl.when(step == pl.num_programs(0) - 1)
    def _():
        store(chunks - 2, width).wait()
        store(chunks - 1, last).wait()
        everything = pl.ds(0, chunks * width)
        ref = incoming.at[pl.ds(0, 15), pl.ds(0, 6), everything]
        pltpu.make_async_copy(ref, ref, send_sem.at[REGROUP]).wait()
        edge, low = sum(cuts), sum(lows)
        counts = {ACROSS: 2 * block, LOW: 2 * block, HIGH: 2 * block}
        counts |= {FAR_LOW: 2 * half, FAR_HIGH: 2 * half}
        counts |= {EDGE_LOW: edge, EDGE_HIGH: edge, EDGE_FAR: edge}
        counts |= {MIX_LOW: 2 * block - edge, MIX_HIGH: 2 * block - edge}
        counts |= {MIXFAR_LOW: low, MIXFAR_HIGH: 2 * block - edge - low}
        for kind, count in counts.items():
            ref = panel.at[pl.ds(0, count), pl.ds(0, chunks // 2 * width)]
            pltpu.make_async_copy(ref, ref, send_sem.at[kind]).wait()
        w_wait(w_send_sem, W_ACROSS, 48)
        w_wait(w_send_sem, W_ALONG, 48 * 6)
        w_wait(w_send_sem, W_CORE, 48 * 8)


def shards(residual, cycle_coupling, pair_amps, occupied_order, virtual_order):
    occupied = occupied_order.shape[0]
    virtual = virtual_order.shape[0]
    local_rows, local_columns = residual.shape
    residual = residual.T
    coupling = cycle_coupling.reshape(local_rows, cycle_coupling.shape[2]).T
    depth = local_rows
    chunks = pl.cdiv(local_columns, LANES)
    padded = chunks * LANES
    columns = local_columns // virtual
    steps = chunks + LAG_MATMUL

    def at(step):
        return jnp.maximum(step - LAG_MATMUL, 0), 0

    def whole(shape):
        return pl.BlockSpec(shape, lambda step: (0, 0))

    anywhere = pl.BlockSpec(memory_space=pl.ANY)
    return pl.pallas_call(
        functools.partial(kernel, chunks),
        grid=(steps,),
        out_shape=pltpu.VMEM(residual.shape, F32),
        in_specs=[
            whole((1, occupied)),
            pl.BlockSpec((virtual,), lambda step: (0,)),
            anywhere,
            anywhere,
            pl.BlockSpec((LANES, local_rows), at),
        ],
        out_specs=anywhere,
        scratch_shapes=[
            pltpu.VMEM(pair_amps.shape, F32),
            pltpu.VMEM((128, 6 * occupied), jnp.int32),
            pltpu.VMEM((virtual, 128), jnp.int32),
            pltpu.VMEM((2, 6 * occupied, virtual), BF16),
            pltpu.VMEM((columns, 256, virtual), BF16),
            pltpu.VMEM((16, 8, padded), F32),
            pltpu.VMEM((16, 8, padded), F32),
            pltpu.VMEM((depth, padded), F32),
            pltpu.VMEM((depth, local_rows), F32),
            pltpu.VMEM((2, 3 * depth, local_rows), BF16),
            pltpu.VMEM((LANES, 3 * depth), BF16),
            pltpu.VMEM((2, LANES, local_rows), F32),
            pltpu.SemaphoreType.DMA((2,)),
            pltpu.SemaphoreType.DMA((2,)),
            pltpu.SemaphoreType.DMA((KINDS,)),
            pltpu.SemaphoreType.DMA((chunks, KINDS)),
            pltpu.SemaphoreType.DMA((3,)),
            pltpu.SemaphoreType.DMA((3,)),
        ],
        compiler_params=pltpu.CompilerParams(
            collective_id=0, has_side_effects=True, vmem_limit_bytes=48 * 2**20
        ),
        cost_estimate=pl.CostEstimate(
            flops=6 * local_rows * depth * local_columns,
            bytes_accessed=8 * local_rows * local_columns,
            transcendentals=0,
        ),
    )(
        occupied_order.reshape(1, occupied),
        virtual_order,
        pair_amps,
        coupling,
        residual,
    ).T


def solution(mesh):
    in_specs = (P("row", "col"), P("row", None, "col"), P(None, ("row", "col")), P(), P())
    out_specs = P("row", "col")
    return jax.shard_map(shards, mesh=mesh, in_specs=in_specs, out_specs=out_specs, check_vma=False)
```

```python
import functools

import jax
import jax.numpy as jnp
from jax import lax
from jax.experimental import pallas as pl
from jax.experimental.pallas import tpu as pltpu
from jax.sharding import PartitionSpec as P

F32 = jnp.float32
BF16 = jnp.bfloat16
MESH = pl.DeviceIdType.MESH

LANES = 512
LAG_REGROUP = 0
CUT_EVEN = 40
CUT_ODD = 48
LAG_FIRST = 1
LAG_SECOND = 2
LAG_MATMUL = 3

REGROUP, ACROSS, LOW, HIGH, FAR_LOW, FAR_HIGH, MIX_LOW, MIX_HIGH, MIXFAR_LOW, MIXFAR_HIGH = range(10)
EDGE_LOW, EDGE_HIGH, EDGE_FAR = range(10, 13)
KINDS = 13
GROUPS = {first: 1 for first in range(8)}
W_ACROSS, W_ALONG, W_CORE = range(3)


def split(x):
    high = x.astype(BF16)
    return high, (x - high.astype(F32)).astype(BF16)


def kernel(
    chunks,
    occupied_ref,
    virtual_ref,
    amps_hbm,
    coupling_hbm,
    residual_ref,
    out_hbm,
    amps,
    distance,
    column,
    stored,
    picked,
    outgoing,
    incoming,
    panel,
    coupling_t,
    weights,
    factors,
    results,
    load_sem,
    store_sem,
    send_sem,
    recv_sem,
    w_send_sem,
    w_recv_sem,
):
    step = pl.program_id(0)
    row = lax.axis_index("row")
    col = lax.axis_index("col")
    z, hi = row // 2, row % 2
    up, down, far = (z + 1) % 4, (z + 3) % 4, (z + 2) % 4
    lo = col // 2 % 2

    def swapped_from(parity):
        return (lo + parity) % 2

    across = (z * 2 + 1 - hi, col)
    above = (up * 2 + hi, col)
    below = (down * 2 + hi, col)
    width = LANES
    block = panel.shape[0] // 8
    blocks, virtual = picked.shape[0], picked.shape[2]
    half = block // 2
    cuts = (CUT_EVEN, CUT_ODD)
    lows = tuple(pl.cdiv(block - cut, 16) * 8 for cut in cuts)

    def lanes(chunk):
        return pl.ds(pl.multiple_of(chunk * width, width), width)

    def remote(src, dst, kind, chunk, where):
        pltpu.make_async_remote_copy(
            src_ref=src,
            dst_ref=dst,
            send_sem=send_sem.at[kind],
            recv_sem=recv_sem.at[chunk, kind],
            device_id=where,
            device_id_type=MESH,
        ).start()

    def rows(owner_z, owner_hi, first, count):
        start = (owner_z * 2 + owner_hi) * block + first
        return pl.ds(pl.multiple_of(start, 8), count)

    def push(owner_z, owner_hi, first, count, kind, chunk, where):
        ref = panel.at[rows(owner_z, owner_hi, first, count), lanes(chunk)]
        remote(ref, ref, kind, chunk, where)

    def arrived(kind, chunk, count):
        ref = panel.at[pl.ds(0, count), lanes(chunk)]
        pltpu.make_async_copy(ref, ref, recv_sem.at[chunk, kind]).wait()

    def pick(j):
        one_hot = (distance[...] == j).astype(F32).astype(BF16)
        for s in range(2):
            picked[j, pl.ds(128 * s, 128), :] = jnp.dot(
                one_hot, stored[s], preferred_element_type=F32
            ).astype(BF16)

    def permute(chunk, spanned=2):
        lane = lax.broadcasted_iota(jnp.int32, (virtual, 128), 1)
        first = (chunk * width) // virtual
        total = jnp.zeros((256, width), F32)
        for n in range(spanned):
            j = jnp.minimum(first + n, blocks - 1)
            gap = lane - column[...]
            shift = (first + n) * virtual - chunk * width
            parts = [
                (gap == shift - start).astype(F32).astype(BF16) for start in range(0, width, 128)
            ]
            total += jnp.dot(
                picked[j], jnp.concatenate(parts, axis=1), preferred_element_type=F32
            )
        values = (total[:128] + total[128:]).reshape(16, 8, width)
        outgoing[:, :, lanes(chunk)] = values
        incoming[col, :, lanes(chunk)] = outgoing[col, :, lanes(chunk)]

    def group_lanes(first):
        return pl.ds(first * width, GROUPS[first] * width)

    def regroup(first):
        for d in range(1, 16):
            other = (col + d) % 16
            crossed = ((other // 2 % 2 != lo) & (swapped_from(first % 2) == 1)).astype(jnp.int32)
            remote(
                outgoing.at[other, pl.ds(0, 6), group_lanes(first)],
                incoming.at[col, pl.ds(0, 6), group_lanes(first)],
                REGROUP,
                first,
                (z * 2 + (hi + crossed) % 2, other),
            )

    def w_wait(sems, kind, count):
        ref = coupling_t.at[pl.ds(0, count)]
        pltpu.make_async_copy(ref, ref, sems.at[kind]).wait()

    def w_send(owner, kind, where):
        ref = coupling_t.at[pl.ds(pl.multiple_of(owner * 48, 16), 48)]
        pltpu.make_async_remote_copy(
            src_ref=ref,
            dst_ref=ref,
            send_sem=w_send_sem.at[kind],
            recv_sem=w_recv_sem.at[kind],
            device_id=where,
            device_id_type=MESH,
        ).start()

    partners = [across, above, below]

    @pl.when(step == 0)
    def _():
        load_amps = pltpu.make_async_copy(amps_hbm, amps, load_sem.at[0])
        load_amps.start()
        own = pl.ds(pl.multiple_of(col * 48, 16), 48)
        load_coupling = pltpu.make_async_copy(coupling_hbm, coupling_t.at[own], load_sem.at[1])
        load_coupling.start()
        barrier = pltpu.get_barrier_semaphore()
        for where in partners:
            pl.semaphore_signal(barrier, inc=1, device_id=where, device_id_type=MESH)
        for d in range(1, 16):
            pl.semaphore_signal(barrier, inc=1, device_id=(row, (col + d) % 16), device_id_type=MESH)
        for n in range(8):
            other = n // 2 * 4 + (1 - lo) * 2 + n % 2
            pl.semaphore_signal(barrier, inc=1, device_id=(across[0], other), device_id_type=MESH)
        r = lax.broadcasted_iota(jnp.int32, (128, 480), 0)
        k = lax.broadcasted_iota(jnp.int32, (128, 480), 1)
        order = jnp.concatenate([occupied_ref[...]] * 6, axis=1)
        distance[...] = jnp.where(r % 8 == k // 80, order - (r // 8) * blocks, -1)
        column[...] = jnp.broadcast_to(virtual_ref[...].reshape(1, virtual), (128, virtual)).T
        load_amps.wait()
        for i in range(6):
            high, low = split(amps[:, i * virtual : (i + 1) * virtual])
            stored[0, pl.ds(80 * i, 80), :] = high
            stored[1, pl.ds(80 * i, 80), :] = low
        pick(0)
        permute(0, pl.cdiv(width, virtual))
        pl.semaphore_wait(barrier, 26)
        regroup(0)
        load_coupling.wait()
        w_send(col, W_ACROSS, (row, col // 4 * 4 + (col + 2) % 4))
        pick(1)
        permute(1)
        regroup(1)
        for d in range(1, 4):
            w_send(col, W_ALONG, (row, (col + 4 * d) % 16))

    chunk_r = step - LAG_REGROUP

    @pl.when((chunk_r >= 0) & (chunk_r < chunks))
    def _():
        for first in GROUPS:

            @pl.when(chunk_r == first)
            def _(first=first):
                ref = incoming.at[pl.ds(0, 15), pl.ds(0, 6), group_lanes(first)]
                pltpu.make_async_copy(ref, ref, recv_sem.at[first, REGROUP]).wait()

        pieces = [incoming[q, :, lanes(chunk_r)][:6] for q in range(16)]
        panel[rows(z, hi, 0, block), lanes(chunk_r)] = jnp.concatenate(pieces, axis=0)
        push(z, hi, 0, block, ACROSS, chunk_r, across)
        push(z, hi, 0, block, LOW, chunk_r, above)
        push(z, hi, 0, block, HIGH, chunk_r, below)

    def first_stage(chunk, cut, low):
        arrived(ACROSS, chunk, block)
        push(z, 1 - hi, cut, block - cut, MIX_LOW, chunk, above)
        push(z, 1 - hi, cut, block - cut, MIX_HIGH, chunk, below)
        arrived(LOW, chunk, block)
        push(down, hi, 0, half, FAR_LOW, chunk, above)
        push(down, hi, 0, cut, EDGE_LOW, chunk, across)
        arrived(HIGH, chunk, block)
        push(up, hi, half, half, FAR_HIGH, chunk, below)
        push(up, hi, 0, cut, EDGE_HIGH, chunk, across)

    def second_stage(chunk, cut, low):
        arrived(MIX_LOW, chunk, block - cut)
        push(down, 1 - hi, cut, low, MIXFAR_LOW, chunk, above)
        arrived(MIX_HIGH, chunk, block - cut)
        push(up, 1 - hi, cut + low, block - cut - low, MIXFAR_HIGH, chunk, below)
        arrived(FAR_LOW, chunk, half)
        push(far, hi, 0, cut, EDGE_FAR, chunk, across)

    def last_stage(chunk, cut, low):
        arrived(FAR_HIGH, chunk, half)
        arrived(EDGE_LOW, chunk, cut)
        arrived(EDGE_HIGH, chunk, cut)
        arrived(EDGE_FAR, chunk, cut)
        arrived(MIXFAR_LOW, chunk, low)
        arrived(MIXFAR_HIGH, chunk, block - cut - low)

    def by_parity(stage, chunk):
        for parity in range(2):

            @pl.when((chunk >= 0) & (chunk < chunks) & (chunk % 2 == parity))
            def _(parity=parity):
                stage(chunk, cuts[parity], lows[parity])

    by_parity(first_stage, step - LAG_FIRST)
    by_parity(second_stage, step - LAG_SECOND)

    @pl.when(step == 0)
    def _():
        pick(2)
        permute(2)
        regroup(2)

    @pl.when(step == 1)
    def _():
        pick(3)
        permute(3)
        regroup(3)
        pick(4)

    @pl.when(step == 2)
    def _():
        permute(4)
        regroup(4)

    @pl.when(step == 3)
    def _():
        permute(5)
        regroup(5)

    @pl.when(step == 4)
    def _():
        permute(6)
        regroup(6)

    @pl.when(step == 5)
    def _():
        permute(7)
        regroup(7)

    @pl.when(step == 0)
    def _():
        w_wait(w_recv_sem, W_ACROSS, 48)
        for d in range(1, 4):
            w_send(col // 4 * 4 + (col + 2) % 4, W_ALONG, (row, (col + 4 * d) % 16))

    @pl.when(step == LAG_MATMUL)
    def _():
        w_wait(w_recv_sem, W_ALONG, 48 * 6)
        where = (row, col // 2 * 2 + 1 - col % 2)
        for n in range(8):
            w_send(n * 2 + col % 2, W_CORE, where)

    @pl.when(step == LAG_MATMUL)
    def _():
        w_wait(w_recv_sem, W_CORE, 48 * 8)
        size = coupling_t.shape[0]
        r = lax.broadcasted_iota(jnp.int32, (block, 1), 0)
        crossing = r // 12 % 2 != lo
        for parity in range(2):
            swap = crossing & ((lo + parity) % 2 == 0)
            for n in range(8):
                mine = coupling_t[n * block : (n + 1) * block]
                twin = coupling_t[(n ^ 1) * block : (n ^ 1) * block + block]
                high, low = split(jnp.where(swap, twin, mine))
                weights[parity, n * block : (n + 1) * block] = high
                weights[parity, size + n * block : size + (n + 1) * block] = low
                weights[parity, 2 * size + n * block : 2 * size + (n + 1) * block] = high

    chunk_m = step - LAG_MATMUL
    last = out_hbm.shape[0] - (chunks - 1) * width

    def store(chunk, count):
        start = pl.multiple_of(chunk * width, width)
        return pltpu.make_async_copy(
            results.at[chunk % 2, pl.ds(0, count)],
            out_hbm.at[pl.ds(start, count)],
            store_sem.at[chunk % 2],
        )

    by_parity(last_stage, chunk_m)

    @pl.when(chunk_m >= 0)
    def _():
        size = panel.shape[0]
        high, low = split(panel[:, lanes(chunk_m)].T)
        factors[:, 0:size] = high
        factors[:, size : 2 * size] = high
        factors[:, 2 * size : 3 * size] = low
        slot = chunk_m % 2

        @pl.when(chunk_m >= 2)
        def _():
            store(chunk_m - 2, width).wait()

        results[slot] = residual_ref[...] + jnp.dot(
            factors[...], weights[slot], preferred_element_type=F32
        )

        @pl.when(chunk_m < chunks - 1)
        def _():
            store(chunk_m, width).start()

        @pl.when(chunk_m == chunks - 1)
        def _():
            store(chunks - 1, last).start()

    @pl.when(step == pl.num_programs(0) - 1)
    def _():
        store(chunks - 2, width).wait()
        store(chunks - 1, last).wait()
        everything = pl.ds(0, chunks * width)
        ref = incoming.at[pl.ds(0, 15), pl.ds(0, 6), everything]
        pltpu.make_async_copy(ref, ref, send_sem.at[REGROUP]).wait()
        edge, low = sum(cuts), sum(lows)
        counts = {ACROSS: 2 * block, LOW: 2 * block, HIGH: 2 * block}
        counts |= {FAR_LOW: 2 * half, FAR_HIGH: 2 * half}
        counts |= {EDGE_LOW: edge, EDGE_HIGH: edge, EDGE_FAR: edge}
        counts |= {MIX_LOW: 2 * block - edge, MIX_HIGH: 2 * block - edge}
        counts |= {MIXFAR_LOW: low, MIXFAR_HIGH: 2 * block - edge - low}
        for kind, count in counts.items():
            ref = panel.at[pl.ds(0, count), pl.ds(0, chunks // 2 * width)]
            pltpu.make_async_copy(ref, ref, send_sem.at[kind]).wait()
        w_wait(w_send_sem, W_ACROSS, 48)
        w_wait(w_send_sem, W_ALONG, 48 * 6)
        w_wait(w_send_sem, W_CORE, 48 * 8)


def shards(residual, cycle_coupling, pair_amps, occupied_order, virtual_order):
    occupied = occupied_order.shape[0]
    virtual = virtual_order.shape[0]
    local_rows, local_columns = residual.shape
    residual = residual.T
    coupling = cycle_coupling.reshape(local_rows, cycle_coupling.shape[2]).T
    depth = local_rows
    chunks = pl.cdiv(local_columns, LANES)
    padded = chunks * LANES
    columns = local_columns // virtual
    steps = chunks + LAG_MATMUL

    def at(step):
        return jnp.maximum(step - LAG_MATMUL, 0), 0

    def whole(shape):
        return pl.BlockSpec(shape, lambda step: (0, 0))

    anywhere = pl.BlockSpec(memory_space=pl.ANY)
    return pl.pallas_call(
        functools.partial(kernel, chunks),
        grid=(steps,),
        out_shape=pltpu.VMEM(residual.shape, F32),
        in_specs=[
            whole((1, occupied)),
            pl.BlockSpec((virtual,), lambda step: (0,)),
            anywhere,
            anywhere,
            pl.BlockSpec((LANES, local_rows), at),
        ],
        out_specs=anywhere,
        scratch_shapes=[
            pltpu.VMEM(pair_amps.shape, F32),
            pltpu.VMEM((128, 6 * occupied), jnp.int32),
            pltpu.VMEM((virtual, 128), jnp.int32),
            pltpu.VMEM((2, 6 * occupied, virtual), BF16),
            pltpu.VMEM((columns, 256, virtual), BF16),
            pltpu.VMEM((16, 8, padded), F32),
            pltpu.VMEM((16, 8, padded), F32),
            pltpu.VMEM((depth, padded), F32),
            pltpu.VMEM((depth, local_rows), F32),
            pltpu.VMEM((2, 3 * depth, local_rows), BF16),
            pltpu.VMEM((LANES, 3 * depth), BF16),
            pltpu.VMEM((2, LANES, local_rows), F32),
            pltpu.SemaphoreType.DMA((2,)),
            pltpu.SemaphoreType.DMA((2,)),
            pltpu.SemaphoreType.DMA((KINDS,)),
            pltpu.SemaphoreType.DMA((chunks, KINDS)),
            pltpu.SemaphoreType.DMA((3,)),
            pltpu.SemaphoreType.DMA((3,)),
        ],
        compiler_params=pltpu.CompilerParams(
            collective_id=0, has_side_effects=True, vmem_limit_bytes=48 * 2**20
        ),
        cost_estimate=pl.CostEstimate(
            flops=6 * local_rows * depth * local_columns,
            bytes_accessed=8 * local_rows * local_columns,
            transcendentals=0,
        ),
    )(
        occupied_order.reshape(1, occupied),
        virtual_order,
        pair_amps,
        coupling,
        residual,
    ).T


def solution(mesh):
    in_specs = (P("row", "col"), P("row", None, "col"), P(None, ("row", "col")), P(), P())
    out_specs = P("row", "col")
    return jax.shard_map(shards, mesh=mesh, in_specs=in_specs, out_specs=out_specs, check_vma=False)
```
